32 devices in a mesh: section: 2 (over y), dp: 4 (over z), head: 4 (over x, core).
Axes of the slice: x: 2, y: 2, z: 4, core: 2. Of those that a mesh axis runs over, the one named last changes fastest.
Arguments:
- block_input: bfloat16 [8192, 512], P('dp'), may hold values from -6 to 6
- cotangent: float32 [8192, 512], P('dp'), may hold values from -6 to 6
- segment_start: int32 [8192], P('dp'), may hold values 0 or 1
- pad_mask: int32 [8192], P('dp'), may hold values 0 or 1
- qkv_weight: bfloat16 [2, 3, 512, 512], P('section', None, None, 'head'), may hold values from -0.25 to 0.25
- out_weight: bfloat16 [2, 512, 512], P('section', 'head'), may hold values from -1 to 1
- up_weight: bfloat16 [2, 512, 2048], P('section', None, 'head'), may hold values from -0.25 to 0.25
- down_weight: bfloat16 [2, 512, 2048], P('section', None, 'head'), may hold values from -0.125 to 0.125
- norm_gain: float32 [2, 2, 512], P('section'), may hold values from 0.5 to 1.5
- norm_bias: float32 [2, 2, 512], P('section'), may hold values from -3 to 3
Outputs:
- activations: float32 [2, 8192, 512], P('section', 'dp')
- input_grad: float32 [2, 8192, 512], P('section', 'dp')
- token_rms: float32 [2, 8192], P('section', 'dp')
- qkv_grad: float32 [2, 3, 512, 512], P('section', None, None, 'head')
- out_grad: float32 [2, 512, 512], P('section', 'head')
- up_grad: float32 [2, 512, 2048], P('section', None, 'head')
- down_grad: float32 [2, 512, 2048], P('section', None, 'head')
- gain_grad: float32 [2, 2, 512], P('section')
- bias_grad: float32 [2, 2, 512], P('section')
The draws below stay inside these ranges and needn't reach their ends.
All inputs are finite; a program needn't handle non-finite values. No bound on the sum of `segment_start` or of `pad_mask` on one device may be relied on, other than what follows from the above.
Results may differ from the reference program's by a relative error of at most 0.019.
Values may be sent and summed in bfloat16 or wider, within the bound.
No kernel may reach another device: no remote copies, remote signals or barrier semaphores. Data moves between devices by JAX's collectives and lax.ppermute only.
A program may use at most 192 MiB of HBM per device.

```python
import jax
import jax.numpy as jnp
from jax import lax

D = 512
H = 8
E = 64
FF = 2048
NMB = 4
SEQ = 1024
MB_LEN = 256
TOKENS = 8192
N_HEAD = 4


def touch_ends(drawn, own_key, smallest, largest):
    spot = [jax.random.randint(jax.random.fold_in(own_key, axis), (), 0, length) for axis, length in enumerate(drawn.shape)]
    main_axis = drawn.shape.index(max(drawn.shape))
    neighbour = spot[:main_axis] + [(spot[main_axis] + 1) % drawn.shape[main_axis]] + spot[main_axis + 1:]
    return drawn.at[tuple(spot)].set(smallest).at[tuple(neighbour)].set(largest)


def levels(key, shape, shards, smallest, largest):
    level = 1.0
    for axis_at, parts in shards:
        steps = jax.random.uniform(jax.random.fold_in(jax.random.fold_in(key, 6), axis_at), (parts,), jnp.float32, smallest / len(shards), largest / len(shards))
        level = level * jnp.repeat(jnp.exp(steps), shape[axis_at] // parts).reshape((-1,) + (1,) * (len(shape) - 1 - axis_at))
    return level


def bell_draw(rng, dims, deviation, reach, shards=(), held_as=jnp.bfloat16):
    level = levels(rng, dims, shards, -0.22, 0.18) if shards else 1.0
    values = jax.random.normal(rng, dims, jnp.float32) * deviation * level
    return jnp.minimum(jnp.maximum(values, -reach), reach).astype(held_as)


def setup_inputs(seed: int = 0) -> dict:
    keys = jax.random.split(jax.random.key(seed), 11)
    block_input = bell_draw(keys[0], (TOKENS, D), 1.0, 6.0, ((0, 4),))
    cotangent = bell_draw(keys[1], (TOKENS, D), 1.0, 6.0, ((0, 4),), jnp.float32)
    segment_start = touch_ends((jax.random.randint(keys[2], (TOKENS,), 0, 160) < 1).astype(jnp.int32), jax.random.fold_in(keys[2], 1), 0, 1)
    pad_mask = touch_ends((jax.random.randint(keys[3], (TOKENS,), 0, 8) < 7).astype(jnp.int32), jax.random.fold_in(keys[3], 1), 0, 1)
    qkv_weight = bell_draw(keys[4], (2, 3, D, H * E), D ** -0.5, 0.25, ((0, 2), (3, 4)))
    out_weight = bell_draw(keys[5], (2, H * E, D), (H * E // 16) ** -0.5, 1.0, ((0, 2), (1, 4)))
    up_weight = bell_draw(keys[6], (2, D, FF), D ** -0.5, 0.25, ((0, 2), (2, 4)))
    down_weight = bell_draw(keys[7], (2, D, FF), FF ** -0.5, 0.125, ((0, 2), (2, 4)))
    norm_gain = jnp.clip(1.0 + 0.1 * jax.random.normal(keys[8], (2, 2, D), jnp.float32), 0.5, 1.5)
    norm_bias = bell_draw(keys[9], (2, 2, D), 0.5, 3.0, ((0, 2),), jnp.float32)
    return dict(block_input=block_input, cotangent=cotangent, segment_start=segment_start, pad_mask=pad_mask, qkv_weight=qkv_weight, out_weight=out_weight, up_weight=up_weight, down_weight=down_weight, norm_gain=norm_gain, norm_bias=norm_bias)


EPS = 1e-05
HIGHEST = lax.Precision.HIGHEST

@jax.custom_vjp
def low(v):
    return lax.optimization_barrier(v.astype(jnp.bfloat16)).astype(jnp.float32)

@jax.custom_vjp
def low_back(v):
    return v

def low_keep(v):
    return (low(v), None)

def low_pass(kept, grad):
    return (grad,)

def back_keep(v):
    return (v, None)

def back_low(kept, grad):
    return (low(grad),)
low.defvjp(low_keep, low_pass)
low_back.defvjp(back_keep, back_low)

def layer_norm(values_in, gain_vec, bias_vec):
    centre = lax.optimization_barrier(jnp.mean(values_in, axis=-1, keepdims=True))
    shifted = values_in - centre
    spread = lax.optimization_barrier(jnp.mean(shifted * shifted, axis=-1, keepdims=True))
    return shifted * lax.rsqrt(spread + EPS) * gain_vec + bias_vec

def feature_map(values_in):
    return jax.nn.elu(values_in) + 1.0

def block_step(carry_in, inputs):
    state_mat, state_sum, last_id = carry_in
    query_feat, key_feat, value_feat, segment_ids = inputs
    positions = jnp.arange(segment_ids.shape[1])
    causal = positions[:, None] >= positions[None, :]
    same_seg = ((segment_ids[:, :, None] == segment_ids[:, None, :]) & causal[None]).astype(jnp.float32)[:, None]
    scores = low_back(jnp.einsum('bhte,bhse->bhts', query_feat, key_feat, precision=HIGHEST) * same_seg)
    carried = (segment_ids == last_id[:, None]).astype(jnp.float32)[:, None, :, None]
    numerator = low_back(jnp.einsum('bhts,bhse->bhte', low(scores), value_feat, precision=HIGHEST) + carried * jnp.einsum('bhte,bhef->bhtf', query_feat, state_mat, precision=HIGHEST))
    denominator = lax.optimization_barrier(jnp.sum(scores, axis=-1, keepdims=True)) + carried * jnp.einsum('bhte,bhe->bht', query_feat, state_sum, precision=HIGHEST)[..., None] + 1.0
    new_last = segment_ids[:, -1]
    keep_flag = (new_last == last_id).astype(jnp.float32)
    tail_mask = (segment_ids == new_last[:, None]).astype(jnp.float32)[:, None, :, None]
    masked_keys = key_feat * tail_mask
    new_mat = keep_flag[:, None, None, None] * state_mat + jnp.einsum('bhse,bhsf->bhef', masked_keys, value_feat, precision=HIGHEST)
    new_sum = keep_flag[:, None, None] * state_sum + lax.optimization_barrier(jnp.sum(masked_keys, axis=2))
    return ((new_mat, new_sum, new_last), numerator / denominator)

def attention(query_feat, key_feat, value_feat, segment_ids):
    row_count = segment_ids.shape[0]

    def split_blocks(flat_rows):
        return jnp.transpose(flat_rows.reshape(row_count, NMB, MB_LEN, H, E), (1, 0, 3, 2, 4))
    id_blocks = jnp.transpose(segment_ids.reshape(row_count, NMB, MB_LEN), (1, 0, 2))
    start = (jnp.zeros((row_count, H, E, E), jnp.float32), jnp.zeros((row_count, H, E), jnp.float32), jnp.full((row_count,), -1, jnp.int32))
    final_carry, outputs = lax.scan(jax.checkpoint(block_step), start, (split_blocks(query_feat), split_blocks(key_feat), split_blocks(value_feat), id_blocks))
    return jnp.transpose(outputs, (1, 0, 3, 2, 4)).reshape(row_count * SEQ, H * E)

def layer_forward(hidden_in, segment_ids, pad_keys, qkv_w, out_w, up_w, down_w, gains, biases):
    head_cols = H * E // N_HEAD
    unit_cols = FF // N_HEAD
    normed = low(layer_norm(hidden_in, gains[0], biases[0]))
    pieces = []
    for group_num in range(N_HEAD):
        shared = low_back(normed)
        pieces.append(jnp.einsum('td,cdj->ctj', shared, qkv_w[:, :, group_num * head_cols:(group_num + 1) * head_cols], precision=HIGHEST))
    projected = low_back(jnp.concatenate(pieces, axis=2))
    queries = low(feature_map(projected[0]))
    key_feat = low(feature_map(projected[1]) * pad_keys[:, None])
    value_feat = low(projected[2])
    mixed_heads = low(attention(queries, key_feat, value_feat, segment_ids))
    attn_sum = jnp.zeros_like(hidden_in)
    for group_num in range(N_HEAD):
        cols_lo = group_num * head_cols
        attn_sum = attn_sum + low(jnp.dot(mixed_heads[:, cols_lo:cols_lo + head_cols], out_w[cols_lo:cols_lo + head_cols], precision=HIGHEST, preferred_element_type=jnp.float32))
    middle = hidden_in + low_back(attn_sum)
    normed_two = low(layer_norm(middle, gains[1], biases[1]))
    ffn_sum = jnp.zeros_like(hidden_in)
    for group_num in range(N_HEAD):
        cols_lo = group_num * unit_cols
        shared = low_back(normed_two)
        up_proj = low_back(jnp.dot(shared, up_w[:, cols_lo:cols_lo + unit_cols], precision=HIGHEST, preferred_element_type=jnp.float32))
        active = low(jax.nn.gelu(up_proj))
        ffn_sum = ffn_sum + low(jnp.einsum('tj,dj->td', active, down_w[:, cols_lo:cols_lo + unit_cols], precision=HIGHEST))
    return middle + low_back(ffn_sum)

def reference(block_input, cotangent, segment_start, pad_mask, qkv_weight, out_weight, up_weight, down_weight, norm_gain, norm_bias):
    segment_ids = jnp.cumsum(segment_start.reshape(-1, SEQ), axis=1).astype(jnp.int32)
    pad_keys = pad_mask.astype(jnp.float32)

    def forward(first_in, offset, qkv_all, out_all, up_all, down_all, gain_all, bias_all):
        first_out = layer_forward(first_in, segment_ids, pad_keys, qkv_all[0], out_all[0], up_all[0], down_all[0], gain_all[0], bias_all[0])
        second_in = low_back(low(first_out)) + offset
        second_out = layer_forward(second_in, segment_ids, pad_keys, qkv_all[1], out_all[1], up_all[1], down_all[1], gain_all[1], bias_all[1])
        return (first_out, second_out)
    first_in = block_input.astype(jnp.float32)
    outputs, pullback = jax.vjp(forward, first_in, jnp.zeros_like(first_in), qkv_weight.astype(jnp.float32), out_weight.astype(jnp.float32), up_weight.astype(jnp.float32), down_weight.astype(jnp.float32), norm_gain.astype(jnp.float32), norm_bias.astype(jnp.float32))
    grads = pullback((jnp.zeros_like(outputs[0]), cotangent.astype(jnp.float32)))
    activations = jnp.stack([outputs[0], outputs[1]])
    input_grad = jnp.stack([grads[0], grads[1]])
    token_rms = jnp.sqrt(lax.optimization_barrier(jnp.mean(activations * activations, axis=-1)) + 1e-06)
    return (activations, input_grad, token_rms, grads[2], grads[3], grads[4], grads[5], grads[6], grads[7])
```

```python
import functools

import jax
import jax.numpy as jnp
from jax import lax
from jax.experimental import pallas as pl
from jax.experimental.pallas import tpu as pltpu
from jax.sharding import PartitionSpec as P

E = 64
SEQ = 1024
LANES = 128
PAIR = 2 * LANES
CHUNK = 128
EPS = 1e-05
F32 = jnp.float32
BF16 = jnp.bfloat16
ROWS = 128
GELU_C = 0.7978845608028654
GELU_A = 0.044715
SPLIT = 1.0 / 32.0
VMEM_LIMIT = 60 * 1024 * 1024

PAD, SEG, CARRY_IN, TAIL_OUT, CARRIED, TAIL = range(6)


def nn(a, b):
    return jnp.dot(a, b, preferred_element_type=F32)


def nt(a, b):
    return lax.dot_general(a, b, (((1,), (1,)), ((), ())), preferred_element_type=F32)


def tn(a, b):
    return lax.dot_general(a, b, (((0,), (0,)), ((), ())), preferred_element_type=F32)


def first_head(shape):
    return lax.broadcasted_iota(jnp.int32, shape, len(shape) - 1) % LANES < E


def diagonal_blocks():
    row = lax.broadcasted_iota(jnp.int32, (LANES, PAIR), 0) < E
    return (row == first_head((LANES, PAIR))).astype(F32)


def split_pair(block):
    in_a = first_head(block.shape)
    zero = jnp.zeros_like(block)
    return jnp.concatenate([jnp.where(in_a, block, zero), jnp.where(in_a, zero, block)], axis=0)


def side(block, fill):
    return jnp.concatenate([block, jnp.full(block.shape, fill, block.dtype)], axis=1)


def normalise(values):
    centre = jnp.mean(values, axis=-1, keepdims=True)
    shifted = values - centre
    scale = lax.rsqrt(jnp.mean(shifted * shifted, axis=-1, keepdims=True) + EPS)
    return shifted * scale, scale


def norm_backward(grad, unit, scale, gain):
    grad_unit = grad * gain
    mean_grad = jnp.mean(grad_unit, axis=-1, keepdims=True)
    mean_dot = jnp.mean(grad_unit * unit, axis=-1, keepdims=True)
    return scale * (grad_unit - mean_grad - unit * mean_dot)


def row_tiles(total, step=ROWS):
    def decorate(body):
        pl.loop(0, total // step)(
            lambda index: body(pl.ds(pl.multiple_of(index * step, step), step))
        )

    return decorate


def chunk_masks(cols_ref, seg_ref, mask, mask_t):
    row = lax.broadcasted_iota(jnp.int32, (CHUNK, CHUNK), 0)
    col = lax.broadcasted_iota(jnp.int32, (CHUNK, CHUNK), 1)
    for chunk in range(cols_ref.shape[0] // CHUNK):
        span = slice(chunk * CHUNK, (chunk + 1) * CHUNK)
        same = cols_ref[span, SEG : SEG + 1] == seg_ref[0:1, span]
        if mask is not None:
            lower = (same & (col <= row)).astype(F32)
            mask[chunk] = jnp.concatenate([lower, lower], axis=1)
        if mask_t is not None:
            upper = (same & (row <= col)).astype(F32)
            mask_t[chunk] = jnp.concatenate([upper, upper], axis=1)


def qkv_kernel(x, gain, bias, cols, w0, w1, w2, w3, fq, fk, vv, state, w, normed, sems):
    copies = [
        pltpu.make_async_copy(part, w.at[:, :, r * LANES : (r + 1) * LANES], sems.at[r])
        for r, part in enumerate((w0, w1, w2, w3))
    ]
    for copy in copies:
        copy.start()
    total = x.shape[0]

    @row_tiles(total)
    def _(rows):
        unit, _ = normalise(x[rows, :].astype(F32))
        normed[rows, :] = (unit * gain[0:1, :] + bias[0:1, :]).astype(BF16)

    for copy in copies:
        copy.wait()

    @row_tiles(total, 256)
    def _(rows):
        block = normed[rows, :]
        query = nn(block, w[0])
        fq[rows, :] = jnp.where(query > 0, query + 1.0, jnp.exp(jnp.minimum(query, 0.0))).astype(BF16)
        key = nn(block, w[1])
        key = jnp.where(key > 0, key + 1.0, jnp.exp(jnp.minimum(key, 0.0)))
        fk[rows, :] = (key * cols[rows, PAD : PAD + 1]).astype(BF16)
        vv[rows, :] = nn(block, w[2]).astype(BF16)

    diag = diagonal_blocks()
    for pair in range(state.shape[0]):
        lanes = slice(pair * LANES, (pair + 1) * LANES)
        tail = (fk[:, lanes] * cols[:, TAIL_OUT : TAIL_OUT + 1].astype(BF16)).astype(BF16)
        state[pair] = (diag * tn(tail, side(vv[:, lanes], 1.0))).astype(BF16)


def attention_forward(fq, fk, vv, start, cols, seg, o, inv_den, states, mask):
    chunk_masks(cols, seg, mask, None)
    diag = diagonal_blocks()

    @pl.loop(0, start.shape[0])
    def _(pair):
        lanes = pl.ds(pl.multiple_of(pair * LANES, LANES), LANES)
        state = start[pair].astype(F32)
        for chunk in range(fq.shape[0] // CHUNK):
            span = slice(chunk * CHUNK, (chunk + 1) * CHUNK)
            query, key, value = fq[span, lanes], fk[span, lanes], vv[span, lanes]
            carried = cols[span, CARRIED : CARRIED + 1]
            tail = cols[span, TAIL : TAIL + 1].astype(BF16)
            state_low = state.astype(BF16)
            if states is not None:
                states[pair, chunk] = state_low
            scores = (nt(query, split_pair(key)) * mask[chunk]).astype(BF16)
            ones = split_pair(jnp.ones_like(value))
            values = jnp.concatenate([split_pair(value), ones], axis=1)
            both = nn(scores, values) + carried * nn(query, state_low)
            inverse = 1.0 / (both[:, LANES:] + 1.0)
            o[span, lanes] = (both[:, :LANES] * inverse).astype(BF16)
            if inv_den is not None:
                inv_den[span, lanes] = inverse
            keep = carried[CHUNK - 1 : CHUNK, :]
            state = keep * state + diag * tn(key * tail, side(value, 1.0))


def start_copies(parts, place, sems, base):
    copies = [
        pltpu.make_async_copy(part, place(r), sems.at[base + r]) for r, part in enumerate(parts)
    ]
    for copy in copies:
        copy.start()
    return copies


def out_and_norm(o, x, out_w, gain, bias, mid, normed_two):
    @row_tiles(o.shape[0], 256)
    def _(rows):
        mid[rows, :] = x[rows, :].astype(F32) + nn(o[rows, :], out_w[...])

    @row_tiles(o.shape[0])
    def _(rows):
        unit, _ = normalise(mid[rows, :])
        normed_two[rows, :] = (unit * gain[1:2, :] + bias[1:2, :]).astype(BF16)


def gelu_parts(up, with_slope):
    square = up * up
    inner = jnp.tanh(GELU_C * up * (1.0 + GELU_A * square))
    half = 0.5 * (1.0 + inner)
    if not with_slope:
        return up * half, None
    slope = half + up * (0.5 * GELU_C) * (1.0 - inner * inner) * (1.0 + 3.0 * GELU_A * square)
    return up * half, slope


def attention_kernel(
    fq, fk, vv, start, cols, seg, x, gain, bias, w0, w1, w2, w3, mid, normed_two, mask, o, w, sems
):
    copies = start_copies(
        (w0, w1, w2, w3), lambda r: w.at[r * LANES : (r + 1) * LANES, :], sems, 0
    )
    attention_forward(fq, fk, vv, start, cols, seg, o, None, None, mask)
    for copy in copies:
        copy.wait()
    out_and_norm(o, x, w, gain, bias, mid, normed_two)


def up_kernel(normed_two, w0, w1, w2, w3, active):
    width = w0.shape[1]
    for r, w in enumerate((w0, w1, w2, w3)):

        @row_tiles(normed_two.shape[0], 256)
        def _(rows, r=r, w=w):
            up = nn(normed_two[rows, :], w[...])
            active[rows, r * width : (r + 1) * width] = gelu_parts(up, False)[0].astype(BF16)


def down_kernel(mid, active, w0, w1, w2, w3, y):
    width = w0.shape[1]

    @row_tiles(mid.shape[0], 256)
    def _(rows):
        total = mid[rows, :]
        for r, w in enumerate((w0, w1, w2, w3)):
            total = total + nt(active[rows, r * width : (r + 1) * width], w[...])
        y[rows, :] = total.astype(BF16)


def block_kernel(
    fq, fk, vv, start, cols, seg, x, gain, bias, *rest
):
    outs, ups, downs = rest[0:4], rest[4:8], rest[8:12]
    y, mid, o, inv_den, states, active, slope = rest[12:19]
    mask, normed_two, out_w, up_w, down_w, sems = rest[19:]
    out_copies = start_copies(
        outs, lambda r: out_w.at[r * LANES : (r + 1) * LANES, :], sems, 0
    )
    up_copies = start_copies(ups, lambda r: up_w.at[r], sems, 4)
    down_copies = start_copies(downs, lambda r: down_w.at[r], sems, 8)
    attention_forward(fq, fk, vv, start, cols, seg, o, inv_den, states, mask)
    for copy in out_copies:
        copy.wait()
    out_and_norm(o, x, out_w, gain, bias, mid, normed_two)
    for copy in up_copies + down_copies:
        copy.wait()
    width = up_w.shape[2]

    @row_tiles(x.shape[0], 256)
    def _(rows):
        total = mid[rows, :]
        for r in range(4):
            units = slice(r * width, (r + 1) * width)
            value, steep = gelu_parts(nn(normed_two[rows, :], up_w[r]), True)
            value = value.astype(BF16)
            active[rows, units] = value
            slope[rows, units] = steep.astype(BF16)
            total = total + nt(value, down_w[r])
        y[rows, :] = total.astype(BF16)


def ffn_back_kernel(with_weights, gy, slope, mid, o, inv_den, fq, cols, gain, *rest):
    outs, ups, downs = rest[0:4], rest[4:8], rest[8:12]
    rest = rest[12:]
    grad_mid, dnum, dden, grad_state = rest[0:4]
    rest = rest[4:]
    if with_weights:
        dup_out, dattn, sums = rest[0:3]
        rest = rest[3:]
    else:
        dattn, rest = rest[0], rest[1:]
    out_w, up_w, down_w, sems = rest
    down_copies = start_copies(downs, lambda r: down_w.at[r], sems, 8)
    up_copies = start_copies(ups, lambda r: up_w.at[r], sems, 4)
    out_copies = start_copies(
        outs, lambda r: out_w.at[r * LANES : (r + 1) * LANES, :], sems, 0
    )
    width = up_w.shape[2]
    total = gy.shape[0]
    for copy in down_copies + up_copies:
        copy.wait()

    @row_tiles(total, 256)
    def _(rows):
        dffn = gy[rows, :].astype(BF16)
        grad = jnp.zeros(gy[rows, :].shape, F32)
        for r in range(4):
            units = slice(r * width, (r + 1) * width)
            dup = (slope[rows, units].astype(F32) * nn(dffn, down_w[r])).astype(BF16)
            if with_weights:
                dup_out[rows, units] = dup
            grad = grad + nt(dup, up_w[r])
        grad_mid[rows, :] = grad

    if with_weights:
        sums[...] = jnp.zeros_like(sums)

    @row_tiles(total)
    def _(rows):
        unit, scale = normalise(mid[rows, :])
        grad = grad_mid[rows, :]
        if with_weights:
            sums[0:1, :] += jnp.sum(grad * unit, axis=0, keepdims=True)
            sums[1:2, :] += jnp.sum(grad, axis=0, keepdims=True)
        grad = gy[rows, :].astype(F32) + norm_backward(grad, unit, scale, gain[1:2, :])
        grad_mid[rows, :] = grad
        dattn[rows, :] = grad.astype(BF16)

    for copy in out_copies:
        copy.wait()

    row_a = lax.broadcasted_iota(jnp.int32, (LANES, LANES), 0) < E
    spread = (row_a == first_head((LANES, LANES))).astype(BF16)
    use_low = lax.broadcasted_iota(jnp.int32, (256, LANES), 1) % E >= E // 2

    @row_tiles(total, 256)
    def _(rows):
        grad_heads = nt(dattn[rows, :], out_w[...])
        scaled = grad_heads * inv_den[rows, :]
        dnum[rows, :] = scaled.astype(BF16)
        product = -scaled * o[rows, :].astype(F32)
        for pair in range(grad_state.shape[0]):
            lanes = slice(pair * LANES, (pair + 1) * LANES)
            part = product[:, lanes]
            high = part.astype(BF16)
            low = (part - high.astype(F32)).astype(BF16)
            whole = nn(high, spread) + nn(low, spread)
            high = whole.astype(BF16)
            low = (whole - high.astype(F32)).astype(BF16)
            dden[rows, lanes] = jnp.where(use_low, low, high)

    diag = diagonal_blocks()
    carry_in = cols[:, CARRY_IN : CARRY_IN + 1].astype(BF16)
    for pair in range(grad_state.shape[0]):
        lanes = slice(pair * LANES, (pair + 1) * LANES)
        both = jnp.concatenate([dnum[:, lanes], dden[:, lanes]], axis=1)
        grad_state[pair] = (diag * tn(fq[:, lanes] * carry_in, both)).astype(BF16)


def attention_back_kernel(
    with_weights, fq, fk, vv, dnum, dden, states, end, cols, seg, x, grad_mid, gain, bias,
    w0, w1, w2, w3, grad_x, dproj, *rest
):
    if with_weights:
        normed, sums = rest[0:2]
        rest = rest[2:]
    mask, mask_t, w, acc, sems = rest
    copies = start_copies(
        (w0, w1, w2, w3), lambda r: w.at[:, :, r * LANES : (r + 1) * LANES], sems, 0
    )
    chunk_masks(cols, seg, mask, mask_t)
    diag = diagonal_blocks()
    lane = lax.broadcasted_iota(jnp.int32, (1, PAIR), 1)
    share = jnp.where(lane < LANES, 1.0, SPLIT)

    @pl.loop(0, end.shape[0])
    def _(pair):
        lanes = pl.ds(pl.multiple_of(pair * LANES, LANES), LANES)
        grad_state = end[pair].astype(F32)
        for chunk in reversed(range(fq.shape[0] // CHUNK)):
            span = slice(chunk * CHUNK, (chunk + 1) * CHUNK)
            query, key, value = fq[span, lanes], fk[span, lanes], vv[span, lanes]
            grad_n, grad_d = dnum[span, lanes], dden[span, lanes]
            carried = cols[span, CARRIED : CARRIED + 1]
            tail = cols[span, TAIL : TAIL + 1]
            keep = carried[CHUNK - 1 : CHUNK, :]
            query_two = split_pair(query)
            grad_n_two = split_pair(grad_n)
            both = jnp.concatenate([grad_n, grad_d], axis=1)
            both_two = jnp.concatenate([grad_n_two, split_pair(grad_d)], axis=1)
            share_two = split_pair(jnp.full(value.shape, SPLIT, BF16))
            values_two = jnp.concatenate([split_pair(value), share_two], axis=1)
            values = side(value, SPLIT)
            scores_t = (nt(key, query_two) * mask_t[chunk]).astype(BF16)
            dscores = (nt(both, values_two) * mask[chunk]).astype(BF16)
            dscores_t = (nt(values, both_two) * mask_t[chunk]).astype(BF16)
            state = (states[pair, chunk].astype(F32) * share).astype(BF16)
            grad_low = grad_state.astype(BF16)
            dfq = nn(dscores, split_pair(key)) + carried * nt(both, state)
            dfk = nn(dscores_t, query_two) + tail * nt(values, grad_low)
            dvv = nn(scores_t, grad_n_two) + tail * nn(key, grad_low[:, :LANES])
            dproj[0, span, lanes] = (jnp.minimum(query.astype(F32), 1.0) * dfq).astype(BF16)
            dproj[1, span, lanes] = (jnp.minimum(key.astype(F32), 1.0) * dfk).astype(BF16)
            dproj[2, span, lanes] = dvv.astype(BF16)
            moved = diag * tn(query * carried.astype(BF16), both)
            grad_state = keep * grad_state + moved

    for copy in copies:
        copy.wait()

    @row_tiles(x.shape[0], 256)
    def _(rows):
        acc[rows, :] = (
            nt(dproj[0, rows, :], w[0]) + nt(dproj[1, rows, :], w[1]) + nt(dproj[2, rows, :], w[2])
        )

    if with_weights:
        sums[...] = jnp.zeros_like(sums)

    @row_tiles(x.shape[0])
    def _(rows):
        unit, scale = normalise(x[rows, :].astype(F32))
        grad = acc[rows, :]
        if with_weights:
            normed[rows, :] = (unit * gain[0:1, :] + bias[0:1, :]).astype(BF16)
            sums[0:1, :] += jnp.sum(grad * unit, axis=0, keepdims=True)
            sums[1:2, :] += jnp.sum(grad, axis=0, keepdims=True)
        grad = grad_mid[rows, :] + norm_backward(grad, unit, scale, gain[0:1, :])
        grad_x[rows, :] = grad.astype(BF16)


def down_grad_kernel(gy, active, keep, send, turned):
    turned[...] = gy[...].astype(BF16).T
    width = active.shape[1] // 4
    for r, (place, slot) in enumerate(((keep, 0), (send, 0), (keep, 1), (send, 1))):
        place[slot] = nn(turned[...], active[:, r * width : (r + 1) * width]).astype(BF16)


def up_grad_kernel(mid, gain, bias, dup, keep, send, normed_two, turned):
    @row_tiles(mid.shape[0])
    def _(rows):
        unit, _ = normalise(mid[rows, :])
        normed_two[rows, :] = (unit * gain[1:2, :] + bias[1:2, :]).astype(BF16)

    turned[...] = normed_two[...].T
    width = dup.shape[1] // 4
    for r, (place, slot) in enumerate(((keep, 0), (send, 0), (keep, 1), (send, 1))):
        place[slot] = nn(turned[...], dup[:, r * width : (r + 1) * width]).astype(BF16)


def late_grad_kernel(normed, dproj, o, dattn, sums_one, sums_two, keep, send, turned):
    width = normed.shape[1]
    base = 3 * width
    last = base + width
    places = ((keep, 0), (send, 0), (keep, 1), (send, 1))
    turned[...] = normed[...].T
    for c in range(3):
        whole = nn(turned[...], dproj[c]).astype(BF16)
        for r, (place, slot) in enumerate(places):
            place[slot, c * width : (c + 1) * width, :] = whole[:, r * LANES : (r + 1) * LANES]
    turned[...] = o[...].T
    for r, (place, slot) in enumerate(places):
        rows = slice(r * LANES, (r + 1) * LANES)
        whole = nn(turned[rows, :], dattn[...]).astype(BF16)
        for n in range(width // LANES):
            to = base + n * LANES
            place[slot, to : to + LANES, :] = whole[:, n * LANES : (n + 1) * LANES]
    four = (sums_one[0:1], sums_two[0:1], sums_one[1:2], sums_two[1:2])
    small = jnp.concatenate(
        [v[:, n * LANES : (n + 1) * LANES] for v in four for n in range(width // LANES)], axis=0
    ).astype(BF16)
    for place, slot in places:
        place[slot, last : last + small.shape[0], :] = small
        left = place.shape[1] - last - small.shape[0]
        place[slot, last + small.shape[0] :, :] = jnp.zeros((left, LANES), BF16)


IN_VMEM = pl.BlockSpec(memory_space=pltpu.VMEM)
ANYWHERE = pl.BlockSpec(memory_space=pl.ANY)


def call(kernel, operands, outputs, scratch, name, gflop, far=()):
    near = [jax.ShapeDtypeStruct(shape, dtype) for shape, dtype in outputs]
    moved = sum(v.size * v.dtype.itemsize for v in (*operands, *far))
    return pl.pallas_call(
        kernel,
        out_shape=near,
        in_specs=[IN_VMEM] * len(operands) + [ANYWHERE] * len(far),
        out_specs=[IN_VMEM] * len(near),
        scratch_shapes=scratch,
        compiler_params=pltpu.CompilerParams(vmem_limit_bytes=VMEM_LIMIT),
        cost_estimate=pl.CostEstimate(
            flops=int(gflop * 1e9), bytes_accessed=int(moved), transcendentals=0
        ),
        name=name,
    )(*operands, *far)


def across(block, distance, axis="head"):
    size = lax.axis_size(axis)
    return lax.ppermute(block, axis, [(i, i ^ distance) for i in range(size)])


def gather_shares(block):
    far = across(block, 2)
    return (block, across(block, 1), far, across(far, 1))


def reduce_shares(keep, send):
    came = across(send, 1)
    pair_sum = keep.astype(F32) + came.astype(F32)
    far = across(pair_sum[1].astype(BF16), 2)
    return (pair_sum[0] + far.astype(F32)).astype(BF16)


def token_table(segment_start, pad_mask, place, tokens, parts):
    row_count = segment_start.shape[0] // SEQ
    ids = jnp.cumsum(segment_start.reshape(row_count, SEQ), axis=1).reshape(-1)
    begin = place * tokens
    own = lax.dynamic_slice(ids, (begin,), (tokens,))
    before = lax.dynamic_slice(ids, (jnp.maximum(begin - 1, 0),), (1,))
    before = jnp.where(place % parts == 0, jnp.full_like(before, -1), before)
    last = own.reshape(-1, CHUNK)[:, -1]
    previous = jnp.concatenate([before, last[:-1]])
    pad = lax.dynamic_slice(pad_mask, (begin,), (tokens,))
    columns = [
        pad,
        own,
        own == before,
        own == last[-1:],
        own == jnp.repeat(previous, CHUNK),
        own == jnp.repeat(last, CHUNK),
    ]
    columns = jnp.stack([c.astype(F32) for c in columns], axis=1)
    rows = jnp.broadcast_to(own.astype(F32)[None], (8, tokens))
    return columns, rows


def local(
    block_input, cotangent, segment_start, pad_mask, qkv_weight, out_weight, up_weight,
    down_weight, norm_gain, norm_bias,
):
    heads = lax.axis_size("head")
    row_count = block_input.shape[0] // SEQ
    parts = heads // row_count
    assert heads == 4 and parts == 2
    tokens = block_input.shape[0] // heads
    width = block_input.shape[1]
    units = up_weight.shape[-1] * heads
    pairs = width // LANES
    chunks = tokens // CHUNK
    section = lax.axis_index("section")
    place = lax.axis_index("head")

    gain, bias = norm_gain[0], norm_bias[0]
    qkv = gather_shares(qkv_weight[0])
    out_w = gather_shares(out_weight[0])
    up_w = gather_shares(up_weight[0])
    down_w = gather_shares(down_weight[0])

    cols, seg = token_table(segment_start, pad_mask, place, tokens, parts)
    own_x = lax.dynamic_slice(block_input, (place * tokens, 0), (tokens, width))
    own_g = lax.dynamic_slice(cotangent, (place * tokens, 0), (tokens, width))

    wide = (tokens, width)
    state_shape = (pairs, LANES, PAIR)
    dma = pltpu.SemaphoreType.DMA
    mask_mem = pltpu.VMEM((chunks, CHUNK, PAIR), F32)
    qkv_mem = pltpu.VMEM((3, width, width), BF16)
    out_mem = pltpu.VMEM((width, width), BF16)
    ffn_mem = pltpu.VMEM((4, width, units // 4), BF16)
    row_mem = pltpu.VMEM(wide, BF16)

    def features(x, name):
        fq, fk, vv, state = call(
            qkv_kernel, (x, gain, bias, cols),
            [(wide, BF16)] * 3 + [(state_shape, BF16)],
            [qkv_mem, row_mem, dma((4,))], name, 0.9, far=qkv,
        )
        came = across(state, 1)
        start = came.reshape(2, 2, LANES, PAIR)[:, ::-1].reshape(state_shape)
        return fq, fk, vv, start

    fq, fk, vv, start = features(own_x, "qkv_first")
    mid, normed_two = call(
        attention_kernel, (fq, fk, vv, start, cols, seg, own_x, gain, bias),
        [(wide, F32), (wide, BF16)],
        [mask_mem, row_mem, out_mem, dma((4,))], "attention_first", 0.8, far=out_w,
    )
    (active,) = call(
        up_kernel, (normed_two, *up_w), [((tokens, units), BF16)], [], "up_first", 1.1
    )
    (y,) = call(down_kernel, (mid, active, *down_w), [(wide, BF16)], [], "down_first", 1.1)
    came = across(y, 1, "section")
    x = jnp.where(section == 0, own_x, came)

    fq, fk, vv, start = features(x, "qkv_second")
    y, mid, o, inv_den, states, active, slope = call(
        block_kernel, (fq, fk, vv, start, cols, seg, x, gain, bias),
        [
            (wide, BF16), (wide, F32), (wide, BF16), (wide, F32),
            ((pairs, chunks, LANES, PAIR), BF16), ((tokens, units), BF16), ((tokens, units), BF16),
        ],
        [mask_mem, row_mem, out_mem, ffn_mem, ffn_mem, dma((12,))],
        "block_second", 3.0, far=(*out_w, *up_w, *down_w),
    )
    activations = lax.all_gather(y, "head", tiled=True).astype(F32)
    token_rms = jnp.sqrt(jnp.mean(activations * activations, axis=-1) + 1e-06)

    def backward(gy, with_weights, name):
        extra = [((tokens, units), BF16), (wide, BF16), ((8, width), F32)] if with_weights else []
        grad_mid, dnum, dden, moved, *saved = call(
            functools.partial(ffn_back_kernel, with_weights),
            (gy, slope, mid, o, inv_den, fq, cols, gain),
            [(wide, F32), (wide, BF16), (wide, BF16), (state_shape, BF16)] + extra,
            ([] if with_weights else [row_mem]) + [out_mem, ffn_mem, ffn_mem, dma((12,))],
            "ffn_back" + name, 2.6, far=(*out_w, *up_w, *down_w),
        )
        came = across(moved, 1)
        end = came.reshape(2, 2, LANES, PAIR)[:, ::-1].reshape(state_shape)
        extra = [(wide, BF16), ((8, width), F32)] if with_weights else []
        grad_x, dproj, *saved_two = call(
            functools.partial(attention_back_kernel, with_weights),
            (fq, fk, vv, dnum, dden, states, end, cols, seg, x, grad_mid, gain, bias),
            [(wide, BF16), ((3, *wide), BF16)] + extra,
            [mask_mem, mask_mem, qkv_mem, pltpu.VMEM(wide, F32), dma((4,))],
            "attention_back" + name, 1.5, far=qkv,
        )
        return grad_x, dproj, saved, saved_two

    grad_x = backward(own_g, False, "_first")[0]
    came = across(grad_x, 1, "section")
    gy = jnp.where(section == 1, own_g, came.astype(F32))

    half = (2, width, units // 4)
    keep, send = call(
        down_grad_kernel, (gy, active), [(half, BF16)] * 2, [row_mem_t(width, tokens)], "down_grad", 1.1
    )
    down_total = reduce_shares(keep, send)
    grad_x, dproj, (dup, dattn, sums_two), (normed, sums_one) = backward(gy, True, "_second")
    keep, send = call(
        up_grad_kernel, (mid, gain, bias, dup), [(half, BF16)] * 2,
        [row_mem, row_mem_t(width, tokens)], "up_grad", 1.1,
    )
    up_total = reduce_shares(keep, send)
    late = 4 * width + 64
    keep, send = call(
        late_grad_kernel, (normed, dproj, o, dattn, sums_one, sums_two),
        [((2, late, LANES), BF16)] * 2, [row_mem_t(width, tokens)], "late_grad", 1.1,
    )
    late_total = reduce_shares(keep, send)
    input_grad = lax.all_gather(grad_x, "head", tiled=True).astype(F32)

    down_total = lax.psum(down_total, "dp").astype(F32)
    up_total = lax.psum(up_total, "dp").astype(F32)
    late_total = lax.psum(late_total, "dp").astype(F32)
    qkv_total = late_total[: 3 * width].reshape(3, width, LANES)
    out_total = late_total[3 * width : 4 * width].reshape(pairs, LANES, LANES)
    out_total = out_total.transpose(1, 0, 2).reshape(LANES, width)
    norm_total = late_total[4 * width : 4 * width + 4 * pairs].reshape(2, 2, width)
    return (
        activations[None], input_grad[None], token_rms[None], qkv_total[None], out_total[None],
        up_total[None], down_total[None], norm_total[0][None], norm_total[1][None],
    )


def row_mem_t(width, tokens):
    return pltpu.VMEM((width, tokens), BF16)


def solution(mesh):
    placed = (
        P("dp", None),
        P("dp", None),
        P("dp"),
        P("dp"),
        P("section", None, None, "head"),
        P("section", "head", None),
        P("section", None, "head"),
        P("section", None, "head"),
        P("section", None, None),
        P("section", None, None),
    )
    return jax.shard_map(
        local,
        mesh=mesh,
        in_specs=placed,
        out_specs=(
            P("section", "dp", None),
            P("section", "dp", None),
            P("section", "dp"),
            P("section", None, None, "head"),
            P("section", "head", None),
            P("section", None, "head"),
            P("section", None, "head"),
            P("section", None, None),
            P("section", None, None),
        ),
        check_vma=False,
    )
```

```python
import functools

import jax
import jax.numpy as jnp
from jax import lax
from jax.experimental import pallas as pl
from jax.experimental.pallas import tpu as pltpu
from jax.sharding import PartitionSpec as P

E = 64
SEQ = 1024
LANES = 128
PAIR = 2 * LANES
CHUNK = 128
EPS = 1e-05
F32 = jnp.float32
BF16 = jnp.bfloat16
ROWS = 128
GELU_C = 0.7978845608028654
GELU_A = 0.044715
SPLIT = 1.0 / 32.0
VMEM_LIMIT = 16 * 1024 * 1024

SECTION, PLACE, DEPTH = range(3)

PAD, SEG, CARRY_IN, TAIL_OUT, CARRIED, TAIL = range(6)


def nn(a, b):
    return jnp.dot(a, b, preferred_element_type=F32)


def nt(a, b):
    return lax.dot_general(a, b, (((1,), (1,)), ((), ())), preferred_element_type=F32)


def tn(a, b):
    return lax.dot_general(a, b, (((0,), (0,)), ((), ())), preferred_element_type=F32)


def first_head(shape):
    return lax.broadcasted_iota(jnp.int32, shape, len(shape) - 1) % LANES < E


def diagonal_blocks():
    row = lax.broadcasted_iota(jnp.int32, (LANES, PAIR), 0) < E
    return (row == first_head((LANES, PAIR))).astype(F32)


def split_pair(block):
    in_a = first_head(block.shape)
    zero = jnp.zeros_like(block)
    return jnp.concatenate([jnp.where(in_a, block, zero), jnp.where(in_a, zero, block)], axis=0)


def side(block, fill):
    return jnp.concatenate([block, jnp.full(block.shape, fill, block.dtype)], axis=1)


def normalise(values):
    centre = jnp.mean(values, axis=-1, keepdims=True)
    shifted = values - centre
    scale = lax.rsqrt(jnp.mean(shifted * shifted, axis=-1, keepdims=True) + EPS)
    return shifted * scale, scale


def norm_backward(grad, unit, scale, gain):
    grad_unit = grad * gain
    mean_grad = jnp.mean(grad_unit, axis=-1, keepdims=True)
    mean_dot = jnp.mean(grad_unit * unit, axis=-1, keepdims=True)
    return scale * (grad_unit - mean_grad - unit * mean_dot)


def row_tiles(total, step=ROWS):
    def decorate(body):
        pl.loop(0, total // step)(
            lambda index: body(pl.ds(pl.multiple_of(index * step, step), step))
        )

    return decorate


def start_copies(parts, place, sems, base):
    copies = [
        pltpu.make_async_copy(part, place(r), sems.at[base + r]) for r, part in enumerate(parts)
    ]
    for copy in copies:
        copy.start()
    return copies


def chunk_masks(cols_ref, seg_ref, mask, mask_t):
    row = lax.broadcasted_iota(jnp.int32, (CHUNK, CHUNK), 0)
    col = lax.broadcasted_iota(jnp.int32, (CHUNK, CHUNK), 1)
    for chunk in range(cols_ref.shape[0] // CHUNK):
        span = slice(chunk * CHUNK, (chunk + 1) * CHUNK)
        same = cols_ref[span, SEG : SEG + 1] == seg_ref[0:1, span]
        if mask is not None:
            lower = (same & (col <= row)).astype(F32)
            mask[chunk] = jnp.concatenate([lower, lower], axis=1)
        if mask_t is not None:
            upper = (same & (row <= col)).astype(F32)
            mask_t[chunk] = jnp.concatenate([upper, upper], axis=1)


def qkv_kernel(second, where, own, *rest):
    if second:
        came, gain, bias, cols, w, fq, fk, vv, state, normed, x_out = rest
        copies = []
    else:
        gain, bias, cols, w0, w1, w2, w3, fq, fk, vv, state, w, normed, sems = rest
        copies = start_copies(
            (w0, w1, w2, w3), lambda r: w.at[:, :, r * LANES : (r + 1) * LANES], sems, 0
        )
    total = own.shape[0]

    @row_tiles(total)
    def _(rows):
        x = own[rows, :].astype(F32)
        if second:
            x = jnp.where(where[SECTION] == 0, x, came[rows, :].astype(F32))
            x_out[rows, :] = x.astype(BF16)
        unit, _ = normalise(x)
        normed[rows, :] = (unit * gain[0:1, :] + bias[0:1, :]).astype(BF16)

    for copy in copies:
        copy.wait()

    @row_tiles(total, 256)
    def _(rows):
        block = normed[rows, :]
        query = nn(block, w[0])
        fq[rows, :] = jnp.where(query > 0, query + 1.0, jnp.exp(jnp.minimum(query, 0.0))).astype(BF16)
        key = nn(block, w[1])
        key = jnp.where(key > 0, key + 1.0, jnp.exp(jnp.minimum(key, 0.0)))
        fk[rows, :] = (key * cols[rows, PAD : PAD + 1]).astype(BF16)
        vv[rows, :] = nn(block, w[2]).astype(BF16)

    diag = diagonal_blocks()
    for pair in range(state.shape[0]):
        lanes = slice(pair * LANES, (pair + 1) * LANES)
        tail = (fk[:, lanes] * cols[:, TAIL_OUT : TAIL_OUT + 1].astype(BF16)).astype(BF16)
        state[pair] = (diag * tn(tail, side(vv[:, lanes], 1.0))).astype(BF16)


def attention_forward(fq, fk, vv, start, cols, seg, o, inv_den, states, mask):
    chunk_masks(cols, seg, mask, None)
    diag = diagonal_blocks()

    @pl.loop(0, start.shape[0])
    def _(pair):
        lanes = pl.ds(pl.multiple_of(pair * LANES, LANES), LANES)
        state = start[pair ^ 1].astype(F32)
        for chunk in range(fq.shape[0] // CHUNK):
            span = slice(chunk * CHUNK, (chunk + 1) * CHUNK)
            query, key, value = fq[span, lanes], fk[span, lanes], vv[span, lanes]
            carried = cols[span, CARRIED : CARRIED + 1]
            tail = cols[span, TAIL : TAIL + 1].astype(BF16)
            state_low = state.astype(BF16)
            if states is not None:
                states[pair, chunk] = state_low
            scores = (nt(query, split_pair(key)) * mask[chunk]).astype(BF16)
            ones = split_pair(jnp.ones_like(value))
            values = jnp.concatenate([split_pair(value), ones], axis=1)
            both = nn(scores, values) + carried * nn(query, state_low)
            inverse = 1.0 / (both[:, LANES:] + 1.0)
            o[span, lanes] = (both[:, :LANES] * inverse).astype(BF16)
            if inv_den is not None:
                inv_den[span, lanes] = inverse
            keep = carried[CHUNK - 1 : CHUNK, :]
            state = keep * state + diag * tn(key * tail, side(value, 1.0))


def out_and_norm(o, x, out_w, gain, bias, mid, normed_two):
    @row_tiles(o.shape[0], 256)
    def _(rows):
        mid[rows, :] = x[rows, :].astype(F32) + nn(o[rows, :], out_w[...])

    @row_tiles(o.shape[0])
    def _(rows):
        unit, _ = normalise(mid[rows, :])
        normed_two[rows, :] = (unit * gain[1:2, :] + bias[1:2, :]).astype(BF16)


def gelu_parts(up, with_slope):
    square = up * up
    inner = jnp.tanh(GELU_C * up * (1.0 + GELU_A * square))
    half = 0.5 * (1.0 + inner)
    if not with_slope:
        return up * half, None
    slope = half + up * (0.5 * GELU_C) * (1.0 - inner * inner) * (1.0 + 3.0 * GELU_A * square)
    return up * half, slope


def attention_kernel(
    fq, fk, vv, start, cols, seg, x, gain, bias, w0, w1, w2, w3, mid, normed_two, w, mask, o, sems
):
    copies = start_copies(
        (w0, w1, w2, w3), lambda r: w.at[r * LANES : (r + 1) * LANES, :], sems, 0
    )
    attention_forward(fq, fk, vv, start, cols, seg, o, None, None, mask)
    for copy in copies:
        copy.wait()
    out_and_norm(o, x, w, gain, bias, mid, normed_two)


def up_kernel(normed_two, w0, w1, w2, w3, active):
    width = w0.shape[1]
    for r, w in enumerate((w0, w1, w2, w3)):

        @row_tiles(normed_two.shape[0], 256)
        def _(rows, r=r, w=w):
            up = nn(normed_two[rows, :], w[...])
            active[rows, r * width : (r + 1) * width] = gelu_parts(up, False)[0].astype(BF16)


def down_kernel(mid, active, w0, w1, w2, w3, y):
    width = w0.shape[1]

    @row_tiles(mid.shape[0], 256)
    def _(rows):
        total = mid[rows, :]
        for r, w in enumerate((w0, w1, w2, w3)):
            total = total + nt(active[rows, r * width : (r + 1) * width], w[...])
        y[rows, :] = total.astype(BF16)


def block_kernel(
    fq, fk, vv, start, cols, seg, x, gain, bias, out_w, u0, u1, u2, u3, d0, d1, d2, d3,
    y, mid, o, o_send, inv_den, states, keep, send, slope, normed_two, mask,
):
    attention_forward(fq, fk, vv, start, cols, seg, o, inv_den, states, mask)
    for slot, r in enumerate((1, 3)):
        o_send[:, slot * LANES : (slot + 1) * LANES] = o[:, r * LANES : (r + 1) * LANES]
    out_and_norm(o, x, out_w, gain, bias, mid, normed_two)
    up_w, down_w = (u0, u1, u2, u3), (d0, d1, d2, d3)
    width = u0.shape[1]

    @row_tiles(x.shape[0], 256)
    def _(rows):
        total = mid[rows, :]
        for r in range(4):
            units = slice(r * width, (r + 1) * width)
            value, steep = gelu_parts(nn(normed_two[rows, :], up_w[r][...]), True)
            value = value.astype(BF16)
            half = slice(r // 2 * width, (r // 2 + 1) * width)
            (send if r % 2 else keep)[rows, half] = value
            slope[rows, units] = steep.astype(BF16)
            total = total + nt(value, down_w[r][...])
        y[rows, :] = total.astype(BF16)


def ffn_back_kernel(with_weights, where, own_g, *rest):
    if with_weights:
        came, rest = rest[0], rest[1:]
    slope, mid, o, inv_den, fq, cols, gain, out_w, *rest = rest
    up_w, down_w = rest[0:4], rest[4:8]
    grad_mid, dnum, dden, grad_state, *rest = rest[8:]
    if with_weights:
        dup_keep, dup_send, dattn, sums, gy = rest
    else:
        (dattn,) = rest
        gy = own_g
    width = up_w[0].shape[1]
    total = gy.shape[0]
    if with_weights:

        @row_tiles(total)
        def _(rows):
            gy[rows, :] = jnp.where(
                where[SECTION] == 1, own_g[rows, :], came[rows, :].astype(F32)
            )

    @row_tiles(total, 256)
    def _(rows):
        dffn = gy[rows, :].astype(BF16)
        grad = jnp.zeros(dffn.shape, F32)
        for r in range(4):
            units = slice(r * width, (r + 1) * width)
            dup = (slope[rows, units].astype(F32) * nn(dffn, down_w[r][...])).astype(BF16)
            if with_weights:
                half = slice(r // 2 * width, (r // 2 + 1) * width)
                (dup_send if r % 2 else dup_keep)[rows, half] = dup
            grad = grad + nt(dup, up_w[r][...])
        grad_mid[rows, :] = grad

    if with_weights:
        sums[...] = jnp.zeros_like(sums)

    @row_tiles(total)
    def _(rows):
        unit, scale = normalise(mid[rows, :])
        grad = grad_mid[rows, :]
        if with_weights:
            sums[0:1, :] += jnp.sum(grad * unit, axis=0, keepdims=True)
            sums[1:2, :] += jnp.sum(grad, axis=0, keepdims=True)
        grad = gy[rows, :] + norm_backward(grad, unit, scale, gain[1:2, :])
        grad_mid[rows, :] = grad
        dattn[rows, :] = grad.astype(BF16)

    row_a = lax.broadcasted_iota(jnp.int32, (LANES, LANES), 0) < E
    spread = (row_a == first_head((LANES, LANES))).astype(BF16)
    use_low = lax.broadcasted_iota(jnp.int32, (256, LANES), 1) % E >= E // 2

    @row_tiles(total, 256)
    def _(rows):
        grad_heads = nt(dattn[rows, :], out_w[...])
        scaled = grad_heads * inv_den[rows, :]
        dnum[rows, :] = scaled.astype(BF16)
        product = -scaled * o[rows, :].astype(F32)
        for pair in range(grad_state.shape[0]):
            lanes = slice(pair * LANES, (pair + 1) * LANES)
            part = product[:, lanes]
            high = part.astype(BF16)
            low = (part - high.astype(F32)).astype(BF16)
            whole = nn(high, spread) + nn(low, spread)
            high = whole.astype(BF16)
            low = (whole - high.astype(F32)).astype(BF16)
            dden[rows, lanes] = jnp.where(use_low, low, high)

    diag = diagonal_blocks()
    carry_in = cols[:, CARRY_IN : CARRY_IN + 1].astype(BF16)
    for pair in range(grad_state.shape[0]):
        lanes = slice(pair * LANES, (pair + 1) * LANES)
        both = jnp.concatenate([dnum[:, lanes], dden[:, lanes]], axis=1)
        grad_state[pair] = (diag * tn(fq[:, lanes] * carry_in, both)).astype(BF16)


def attention_back_kernel(
    with_weights, fq, fk, vv, dnum, dden, states, end, cols, seg, x, grad_mid, gain, w, *rest
):
    if with_weights:
        sums_two, grad_x, keep, send, sums, *rest = rest
    else:
        grad_x, *rest = rest
    mask, mask_t, acc, dproj = rest
    chunk_masks(cols, seg, mask, mask_t)
    diag = diagonal_blocks()
    lane = lax.broadcasted_iota(jnp.int32, (1, PAIR), 1)
    share = jnp.where(lane < LANES, 1.0, SPLIT)

    @pl.loop(0, end.shape[0])
    def _(pair):
        lanes = pl.ds(pl.multiple_of(pair * LANES, LANES), LANES)
        grad_state = end[pair ^ 1].astype(F32)
        for chunk in reversed(range(fq.shape[0] // CHUNK)):
            span = slice(chunk * CHUNK, (chunk + 1) * CHUNK)
            query, key, value = fq[span, lanes], fk[span, lanes], vv[span, lanes]
            grad_n, grad_d = dnum[span, lanes], dden[span, lanes]
            carried = cols[span, CARRIED : CARRIED + 1]
            tail = cols[span, TAIL : TAIL + 1]
            stays = carried[CHUNK - 1 : CHUNK, :]
            query_two = split_pair(query)
            grad_n_two = split_pair(grad_n)
            both = jnp.concatenate([grad_n, grad_d], axis=1)
            both_two = jnp.concatenate([grad_n_two, split_pair(grad_d)], axis=1)
            share_two = split_pair(jnp.full(value.shape, SPLIT, BF16))
            values_two = jnp.concatenate([split_pair(value), share_two], axis=1)
            values = side(value, SPLIT)
            scores_t = (nt(key, query_two) * mask_t[chunk]).astype(BF16)
            dscores = (nt(both, values_two) * mask[chunk]).astype(BF16)
            dscores_t = (nt(values, both_two) * mask_t[chunk]).astype(BF16)
            state = (states[pair, chunk].astype(F32) * share).astype(BF16)
            grad_low = grad_state.astype(BF16)
            dfq = nn(dscores, split_pair(key)) + carried * nt(both, state)
            dfk = nn(dscores_t, query_two) + tail * nt(values, grad_low)
            dvv = nn(scores_t, grad_n_two) + tail * nn(key, grad_low[:, :LANES])
            dproj[0, span, lanes] = (jnp.minimum(query.astype(F32), 1.0) * dfq).astype(BF16)
            dproj[1, span, lanes] = (jnp.minimum(key.astype(F32), 1.0) * dfk).astype(BF16)
            dproj[2, span, lanes] = dvv.astype(BF16)
            moved = diag * tn(query * carried.astype(BF16), both)
            grad_state = stays * grad_state + moved

    @row_tiles(x.shape[0], 256)
    def _(rows):
        acc[rows, :] = (
            nt(dproj[0, rows, :], w[0]) + nt(dproj[1, rows, :], w[1]) + nt(dproj[2, rows, :], w[2])
        )

    if with_weights:
        for r in range(4):
            half = slice(r // 2 * LANES, (r // 2 + 1) * LANES)
            (send if r % 2 else keep)[:, :, half] = dproj[:, :, r * LANES : (r + 1) * LANES]
        sums[...] = jnp.zeros_like(sums)
        sums[1:2, :] = sums_two[0:1, :]
        sums[3:4, :] = sums_two[1:2, :]

    @row_tiles(x.shape[0])
    def _(rows):
        unit, scale = normalise(x[rows, :].astype(F32))
        grad = acc[rows, :]
        if with_weights:
            sums[0:1, :] += jnp.sum(grad * unit, axis=0, keepdims=True)
            sums[2:3, :] += jnp.sum(grad, axis=0, keepdims=True)
        grad = grad_mid[rows, :] + norm_backward(grad, unit, scale, gain[0:1, :])
        grad_x[rows, :] = grad.astype(BF16)


def down_grad_kernel(where, own_g, other_g, came, came_two, own, other, keep, send, turned):
    total = own_g.shape[0]
    for n, (mine, arrived) in enumerate(((own_g, came), (other_g, came_two))):
        whole = jnp.where(where[SECTION] == 1, mine[...], arrived[...].astype(F32))
        turned[:, n * total : (n + 1) * total] = whole.astype(BF16).T
    width = keep.shape[1]
    for r, place in enumerate((keep, send)):
        cols = slice(r * width, (r + 1) * width)
        sum_own = nn(turned[:, :total], own[:, cols])
        place[...] = (sum_own + nn(turned[:, total:], other[:, cols])).astype(BF16)


def up_grad_kernel(normed_own, normed_other, own, other, keep, send, turned):
    total = normed_own.shape[0]
    turned[:, :total] = normed_own[...].T
    turned[:, total:] = normed_other[...].T
    width = keep.shape[1]
    for r, place in enumerate((keep, send)):
        cols = slice(r * width, (r + 1) * width)
        sum_own = nn(turned[:, :total], own[:, cols])
        place[...] = (sum_own + nn(turned[:, total:], other[:, cols])).astype(BF16)


def late_grad_kernel(
    normed_own, normed_other, own, other, o_own, o_other, dattn_own, dattn_other,
    sums_own, sums_other, keep, send, turned,
):
    total, width = normed_own.shape
    base = 3 * width
    last = base + width
    places = (keep, send)
    turned[:, :total] = normed_own[...].T
    turned[:, total:] = normed_other[...].T
    for c in range(3):
        whole = nn(turned[:, :total], own[c]) + nn(turned[:, total:], other[c])
        for r, place in enumerate(places):
            cols = slice(r * LANES, (r + 1) * LANES)
            place[c * width : (c + 1) * width, :] = whole[:, cols].astype(BF16)
    for r, place in enumerate(places):
        here = o_own[:, 2 * r * LANES : (2 * r + 1) * LANES].T
        there = o_other[:, r * LANES : (r + 1) * LANES].T
        whole = (nn(here, dattn_own[...]) + nn(there, dattn_other[...])).astype(BF16)
        for n in range(width // LANES):
            to = base + n * LANES
            place[to : to + LANES, :] = whole[:, n * LANES : (n + 1) * LANES]
    four = sums_own[0:4, :] + sums_other[0:4, :]
    small = jnp.concatenate(
        [four[v : v + 1, n * LANES : (n + 1) * LANES] for v in range(4) for n in range(width // LANES)],
        axis=0,
    ).astype(BF16)
    for place in places:
        place[last : last + small.shape[0], :] = small
        left = place.shape[0] - last - small.shape[0]
        place[last + small.shape[0] :, :] = jnp.zeros((left, LANES), BF16)


def part_rows(where, r, size):
    return pl.ds(pl.multiple_of((where[DEPTH] ^ r) * size, 16), size)


def cut_kernel(where, keep, came, *outs):
    for r, out in enumerate(outs):
        rows = part_rows(where, r, out.shape[0])
        total = keep[rows, :].astype(F32) + came[rows, :].astype(F32)
        out[...] = total.astype(out.dtype)


def add_kernel(own, one, two, three, out):
    total = own[...] + one[...].astype(F32) + two[...].astype(F32) + three[...].astype(F32)
    out[...] = total.astype(BF16)


def join_kernel(where, own, one, two, three, out):
    for r, part in enumerate((own, one, two, three)):
        out[part_rows(where, r, part.shape[0]), :] = part[...].astype(F32)


def unpack_late(source, qkv, out, gains, biases):
    width = out.shape[1]
    base = 3 * width
    last = base + width
    pairs = width // LANES
    for c in range(3):
        qkv[c] = source[c * width : (c + 1) * width, :].astype(F32)
    for n in range(pairs):
        cols = slice(n * LANES, (n + 1) * LANES)
        out[:, cols] = source[base + n * LANES : base + (n + 1) * LANES, :].astype(F32)
        for v, place in enumerate((gains, gains, biases, biases)):
            row = last + v * pairs + n
            place[v % 2 : v % 2 + 1, cols] = source[row : row + 1, :].astype(F32)


def join_late_kernel(where, own, one, two, three, qkv, out, gains, biases, whole):
    join_kernel(where, own, one, two, three, whole)
    unpack_late(whole, qkv, out, gains, biases)


def unpack_late_kernel(source, qkv, out, gains, biases, whole):
    whole[...] = source[...].astype(F32)
    unpack_late(whole, qkv, out, gains, biases)


def halves(where):
    depth = where[DEPTH]
    return (depth ^ (depth >> 1)) & 1, depth >> 1


def rows_at(index, size):
    return pl.ds(pl.multiple_of(index * size, 16), size)


def halve_first_kernel(where, keep, came, stays, goes):
    mine, _ = halves(where)
    size = stays.shape[0]
    for index, out in ((mine, stays), (1 - mine, goes)):
        rows = rows_at(index, size)
        out[...] = (keep[rows, :].astype(F32) + came[rows, :].astype(F32)).astype(out.dtype)


def halve_second_kernel(where, keep, came, stays, goes):
    _, mine = halves(where)
    size = stays.shape[0]
    for index, out in ((mine, stays), (1 - mine, goes)):
        rows = rows_at(index, size)
        out[...] = (keep[rows, :] + came[rows, :].astype(F32)).astype(out.dtype)


def sum_kernel(keep, came, out):
    out[...] = (keep[...] + came[...].astype(F32)).astype(BF16)


def pair_kernel(where, own, came, out):
    _, mine = halves(where)
    size = own.shape[0]
    out[rows_at(mine, size), :] = own[...]
    out[rows_at(1 - mine, size), :] = came[...]


def whole_kernel(where, own, came, out):
    mine, _ = halves(where)
    size = own.shape[0]
    out[rows_at(mine, size), :] = own[...].astype(F32)
    out[rows_at(1 - mine, size), :] = came[...].astype(F32)


def finish_kernel(with_rms, where, p0, p1, p2, p3, out, *rms):
    total, width = p0.shape
    for r, part in enumerate((p0, p1, p2, p3)):
        begin = where[PLACE] ^ r

        @pl.loop(0, total // LANES)
        def _(tile, part=part, begin=begin):
            block = part[pl.ds(pl.multiple_of(tile * LANES, LANES), LANES), :].astype(F32)
            to = begin * (total // LANES) + tile
            out[pl.ds(pl.multiple_of(to * LANES, LANES), LANES), :] = block
            if with_rms:
                square = block * block
                high = square.astype(BF16)
                low = (square - high.astype(F32)).astype(BF16)
                ones = jnp.ones((8, width), BF16)
                mean = (nt(ones, high) + nt(ones, low)) * (1.0 / width)
                rms[0][pl.ds(to, 1), :] = jnp.sqrt(mean[0:1, :] + 1e-06)


IN_VMEM = pl.BlockSpec(memory_space=pltpu.VMEM)
IN_SMEM = pl.BlockSpec(memory_space=pltpu.SMEM)
ANYWHERE = pl.BlockSpec(memory_space=pl.ANY)


def call(kernel, operands, outputs, scratch, name, us, far=()):
    near = [jax.ShapeDtypeStruct(shape, dtype) for shape, dtype in outputs]
    return pl.pallas_call(
        kernel,
        out_shape=near,
        in_specs=[IN_SMEM if v.dtype == jnp.int32 else IN_VMEM for v in operands]
        + [ANYWHERE] * len(far),
        out_specs=[IN_VMEM] * len(near),
        scratch_shapes=scratch,
        compiler_params=pltpu.CompilerParams(vmem_limit_bytes=VMEM_LIMIT),
        cost_estimate=pl.CostEstimate(
            flops=int(us * 1.1e9), bytes_accessed=0, transcendentals=0
        ),
        name=name,
    )(*operands, *far)


def across(block, distance, axis="head"):
    size = lax.axis_size(axis)
    return lax.ppermute(block, axis, [(i, i ^ distance) for i in range(size)])


def spread(block, far):
    return (block, across(block, 1), far, across(far, 1))


def after(value, *others):
    return lax.optimization_barrier((value, *others))[0]


def sum_rows(keep, send, where, join, name):
    came = across(send, 2)
    rows, width = keep.shape
    depth = lax.axis_size("dp")
    if depth != 4:
        total = (keep.astype(F32) + came.astype(F32)).astype(BF16)
        return join(where, lax.psum(total, "dp"))
    part = (rows // depth, width)
    own, *parts = call(
        cut_kernel, (where, keep, came), [(part, F32)] + [(part, BF16)] * 3, [], "cut" + name, 0.7
    )
    parts = [across(v, r + 1, "dp") for r, v in enumerate(parts)]
    (own,) = call(add_kernel, (own, *parts), [(part, BF16)], [], "add" + name, 0.7)
    return join(where, own, *[across(own, r, "dp") for r in (1, 2, 3)])


def halving_sum(keep, came, where, name):
    rows, width = keep.shape
    if lax.axis_size("dp") != 4:
        total = (keep.astype(F32) + came.astype(F32)).astype(BF16)
        yield total
        yield total
        yield lax.psum(total, "dp").astype(F32)
        return
    half, quarter = (rows // 2, width), (rows // 4, width)
    stays, goes = call(
        halve_first_kernel, (where, keep, came), [(half, F32), (half, BF16)], [], "halve_" + name, 0.8
    )
    came = across(goes, 1, "dp")
    yield goes
    stays, goes = call(
        halve_second_kernel, (where, stays, came), [(quarter, F32), (quarter, BF16)], [],
        "halve_again_" + name, 0.7,
    )
    came = across(goes, 3, "dp")
    yield goes
    (own,) = call(sum_kernel, (stays, came), [(quarter, BF16)], [], "sum_" + name, 0.6)
    came = across(own, 3, "dp")
    (own,) = call(pair_kernel, (where, own, came), [(half, BF16)], [], "pair_" + name, 0.6)
    came = across(own, 1, "dp")
    yield call(whole_kernel, (where, own, came), [((rows, width), F32)], [], "whole_" + name, 1.0)[0]


def finish(where, own, far, with_rms, name):
    rows, width = own.shape[0] * 4, own.shape[1]
    outputs = [((rows, width), F32)] + [((rows // LANES, LANES), F32)] * with_rms
    return call(
        functools.partial(finish_kernel, with_rms),
        (where, own, across(own, 1), far, across(far, 1)), outputs, [], name, 3.0,
    )


def token_table(segment_start, pad_mask, place, tokens, parts):
    row_count = segment_start.shape[0] // SEQ
    ids = jnp.cumsum(segment_start.reshape(row_count, SEQ), axis=1).reshape(-1)
    begin = place * tokens
    own = lax.dynamic_slice(ids, (begin,), (tokens,))
    before = lax.dynamic_slice(ids, (jnp.maximum(begin - 1, 0),), (1,))
    before = jnp.where(place % parts == 0, jnp.full_like(before, -1), before)
    last = own.reshape(-1, CHUNK)[:, -1]
    previous = jnp.concatenate([before, last[:-1]])
    pad = lax.dynamic_slice(pad_mask, (begin,), (tokens,))
    columns = [
        pad,
        own,
        own == before,
        own == last[-1:],
        own == jnp.repeat(previous, CHUNK),
        own == jnp.repeat(last, CHUNK),
    ]
    columns = jnp.stack([c.astype(F32) for c in columns], axis=1)
    rows = jnp.broadcast_to(own.astype(F32)[None], (8, tokens))
    return columns, rows


def local(
    block_input, cotangent, segment_start, pad_mask, qkv_weight, out_weight, up_weight,
    down_weight, norm_gain, norm_bias,
):
    heads = lax.axis_size("head")
    row_count = block_input.shape[0] // SEQ
    parts = heads // row_count
    assert heads == 4 and parts == 2
    tokens = block_input.shape[0] // heads
    width = block_input.shape[1]
    units = up_weight.shape[-1] * heads
    pairs = width // LANES
    chunks = tokens // CHUNK
    section = lax.axis_index("section")
    place = lax.axis_index("head")

    gain, bias = norm_gain[0], norm_bias[0]
    far_out = across(out_weight[0], 2)
    far_up = across(up_weight[0], 2)
    far_down = across(down_weight[0], 2)

    cols, seg = token_table(segment_start, pad_mask, place, tokens, parts)
    own_x = lax.dynamic_slice(block_input, (place * tokens, 0), (tokens, width))

    wide = (tokens, width)
    state_shape = (pairs, LANES, PAIR)
    dma = pltpu.SemaphoreType.DMA
    mask_mem = pltpu.VMEM((chunks, CHUNK, PAIR), F32)
    row_mem = pltpu.VMEM(wide, BF16)

    own_g = lax.dynamic_slice(cotangent, (place * tokens, 0), (tokens, width))
    other_g = lax.dynamic_slice(cotangent, ((place ^ 1) * tokens, 0), (tokens, width))
    where = jnp.stack([section, place, lax.axis_index("dp")]).astype(jnp.int32)
    turned_mem = pltpu.VMEM((width, 2 * tokens), BF16)
    grad_mem = pltpu.VMEM(wide, F32)
    half = (tokens, units // 2)
    features = [(wide, BF16)] * 3 + [(state_shape, BF16)]

    fq, fk, vv, state, qkv = call(
        functools.partial(qkv_kernel, False),
        (where, after(own_x, own_g, other_g, seg), gain, bias, cols),
        features + [((3, width, width), BF16)],
        [row_mem, dma((4,))], "qkv_first", 4.0, far=spread(qkv_weight[0], across(qkv_weight[0], 2)),
    )
    start = across(state, 1)
    mid, normed_two, out_w = call(
        attention_kernel, (fq, fk, vv, start, cols, seg, own_x, gain, bias),
        [(wide, F32), (wide, BF16), ((width, width), BF16)],
        [mask_mem, row_mem, dma((4,))], "attention_first", 5.5,
        far=spread(out_weight[0], after(far_out, fq)),
    )
    up_w = spread(up_weight[0], after(far_up, fq))
    (active,) = call(
        up_kernel, (normed_two, *up_w), [((tokens, units), BF16)], [], "up_first", 3.2
    )
    down_w = spread(down_weight[0], after(far_down, normed_two))
    (y,) = call(down_kernel, (mid, active, *down_w), [(wide, BF16)], [], "down_first", 2.8)
    came = across(y, 1, "section")

    fq, fk, vv, state, normed, x = call(
        functools.partial(qkv_kernel, True), (where, own_x, came, gain, bias, cols, qkv),
        features + [(wide, BF16)] * 2, [], "qkv_second", 3.5,
    )
    start = across(state, 1)
    y, mid, o, o_send, inv_den, states, active, active_send, slope, normed_two = call(
        block_kernel, (fq, fk, vv, start, cols, seg, x, gain, bias, out_w, *up_w, *down_w),
        [
            (wide, BF16), (wide, F32), (wide, BF16), ((tokens, width // 2), BF16), (wide, F32),
            ((pairs, chunks, LANES, PAIR), BF16), (half, BF16), (half, BF16),
            ((tokens, units), BF16), (wide, BF16),
        ],
        [mask_mem], "block_second", 10.0,
    )
    far_y = across(y, 2)
    active_two = across(active_send, 1)
    normed_other = across(normed, 1)
    normed_two_other = across(normed_two, 1)
    o_other = across(o_send, 1)

    def ffn_back(grads, name):
        second = len(grads) > 1
        extra = [(half, BF16)] * 2 + [(wide, BF16), ((2, width), F32)] if second else []
        return call(
            functools.partial(ffn_back_kernel, second),
            (where, *grads, slope, mid, o, inv_den, fq, cols, gain, out_w, *up_w, *down_w),
            [(wide, F32), (wide, BF16), (wide, BF16), (state_shape, BF16)] + extra,
            [grad_mem] if second else [row_mem], name, 7.5,
        )

    def attention_back(sums, grad_mid, dnum, dden, end, name):
        third = ((3, tokens, width // 2), BF16)
        extra = [third, third, ((8, width), F32)] if sums else []
        return call(
            functools.partial(attention_back_kernel, bool(sums)),
            (fq, fk, vv, dnum, dden, states, end, cols, seg, x, grad_mid, gain, qkv, *sums),
            [(wide, BF16)] + extra,
            [mask_mem, mask_mem, grad_mem, pltpu.VMEM((3, *wide), BF16)], name, 7.5,
        )

    grad_mid, dnum, dden, moved = ffn_back((own_g,), "ffn_back_first")
    (grad_x,) = attention_back((), grad_mid, dnum, dden, across(moved, 1), "attention_back_first")
    came = across(grad_x, 1, "section")
    activations, token_rms = finish(
        where, after(y, grad_x), after(far_y, grad_x), True, "activations"
    )
    came = after(came, activations)

    share = (width, units // 4)
    keep, send = call(
        down_grad_kernel, (where, own_g, other_g, came, across(came, 1), active, active_two),
        [(share, BF16)] * 2, [turned_mem], "down_grad", 2.2,
    )
    down_keep, down_far = keep, across(send, 2)
    grad_mid, dnum, dden, moved, dup, dup_send, dattn, sums_two = ffn_back(
        (own_g, after(came, send)), "ffn_back_second"
    )
    end = across(moved, 1)
    dattn_other = across(dattn, 1)
    keep, send = call(
        up_grad_kernel, (normed_two, normed_two_other, dup, across(dup_send, 1)),
        [(share, BF16)] * 2, [turned_mem], "up_grad", 1.3,
    )
    up_keep, up_far = keep, across(send, 2)
    down_steps = halving_sum(down_keep, after(down_far, send), where, "down")
    goes = next(down_steps)
    grad_x, dproj, dproj_send, sums = attention_back(
        (sums_two,), grad_mid, dnum, dden, after(end, goes), "attention_back_second"
    )
    goes = next(down_steps)
    late = (4 * width + 64, LANES)
    keep, send = call(
        late_grad_kernel,
        (
            normed, normed_other, dproj, across(dproj_send, 1), o, o_other, dattn, dattn_other,
            after(sums, goes), across(sums, 1),
        ),
        [(late, BF16)] * 2, [turned_mem], "late_grad", 1.3,
    )
    up_steps = halving_sum(up_keep, after(up_far, grad_x), where, "up")
    next(up_steps)
    next(up_steps)

    def late_join(where, *parts):
        results = [
            ((3, width, LANES), F32), ((LANES, width), F32), ((2, width), F32), ((2, width), F32)
        ]
        if len(parts) == 1:
            kernel, operands = unpack_late_kernel, parts
        else:
            kernel, operands = join_late_kernel, (where, *parts)
        return call(kernel, operands, results, [pltpu.VMEM(late, F32)], "join_late", 1.5)

    qkv_total, out_total, gain_total, bias_total = sum_rows(keep, send, where, late_join, "_late")
    down_total, up_total = next(down_steps), next(up_steps)
    own = after(grad_x, send)
    (input_grad,) = finish(where, own, across(own, 2), False, "input_grad")
    return (
        activations[None], input_grad[None], token_rms.reshape(1, -1), qkv_total[None],
        out_total[None], up_total[None], down_total[None], gain_total[None], bias_total[None],
    )


def solution(mesh):
    placed = (
        P("dp", None),
        P("dp", None),
        P("dp"),
        P("dp"),
        P("section", None, None, "head"),
        P("section", "head", None),
        P("section", None, "head"),
        P("section", None, "head"),
        P("section", None, None),
        P("section", None, None),
    )
    return jax.shard_map(
        local,
        mesh=mesh,
        in_specs=placed,
        out_specs=(
            P("section", "dp", None),
            P("section", "dp", None),
            P("section", "dp"),
            P("section", None, None, "head"),
            P("section", "head", None),
            P("section", None, "head"),
            P("section", None, "head"),
            P("section", None, None),
            P("section", None, None),
        ),
        check_vma=False,
    )
```

```python
import functools

import jax
import jax.numpy as jnp
from jax import lax
from jax.experimental import pallas as pl
from jax.experimental.pallas import tpu as pltpu
from jax.sharding import PartitionSpec as P

E = 64
SEQ = 1024
LANES = 128
PAIR = 2 * LANES
CHUNK = 128
EPS = 1e-05
F32 = jnp.float32
BF16 = jnp.bfloat16
ROWS = 128
GELU_C = 0.7978845608028654
GELU_A = 0.044715
SPLIT = 1.0 / 32.0
LOW = 0.02
VMEM_LIMIT = 16 * 1024 * 1024

SECTION, PLACE, DEPTH = range(3)

PAD, SEG, CARRY_IN, TAIL_OUT, CARRIED, TAIL = range(6)


def nn(a, b):
    return jnp.dot(a, b, preferred_element_type=F32)


def nt(a, b):
    return lax.dot_general(a, b, (((1,), (1,)), ((), ())), preferred_element_type=F32)


def tn(a, b):
    return lax.dot_general(a, b, (((0,), (0,)), ((), ())), preferred_element_type=F32)


def first_head(shape):
    return lax.broadcasted_iota(jnp.int32, shape, len(shape) - 1) % LANES < E


def diagonal_blocks():
    row = lax.broadcasted_iota(jnp.int32, (LANES, PAIR), 0) < E
    return (row == first_head((LANES, PAIR))).astype(F32)


def split_pair(block):
    in_a = first_head(block.shape)
    zero = jnp.zeros_like(block)
    return jnp.concatenate([jnp.where(in_a, block, zero), jnp.where(in_a, zero, block)], axis=0)


def side(block, fill):
    return jnp.concatenate([block, jnp.full(block.shape, fill, block.dtype)], axis=1)


def normalise(values):
    centre = jnp.mean(values, axis=-1, keepdims=True)
    shifted = values - centre
    scale = lax.rsqrt(jnp.mean(shifted * shifted, axis=-1, keepdims=True) + EPS)
    return shifted * scale, scale


def norm_backward(grad, unit, scale, gain):
    grad_unit = grad * gain
    mean_grad = jnp.mean(grad_unit, axis=-1, keepdims=True)
    mean_dot = jnp.mean(grad_unit * unit, axis=-1, keepdims=True)
    return scale * (grad_unit - mean_grad - unit * mean_dot)


def row_tiles(total, step=ROWS):
    def decorate(body):
        pl.loop(0, total // step, unroll=True)(
            lambda index: body(pl.ds(pl.multiple_of(index * step, step), step))
        )

    return decorate


def start_copies(parts, place, sems, base):
    copies = [
        pltpu.make_async_copy(part, place(r), sems.at[base + r]) for r, part in enumerate(parts)
    ]
    for copy in copies:
        copy.start()
    return copies


def chunk_masks(cols_ref, seg_ref, mask, mask_t):
    row = lax.broadcasted_iota(jnp.int32, (CHUNK, CHUNK), 0)
    col = lax.broadcasted_iota(jnp.int32, (CHUNK, CHUNK), 1)
    for chunk in range(cols_ref.shape[0] // CHUNK):
        span = slice(chunk * CHUNK, (chunk + 1) * CHUNK)
        same = cols_ref[span, SEG : SEG + 1] == seg_ref[0:1, span]
        if mask is not None:
            lower = (same & (col <= row)).astype(F32).astype(BF16)
            mask[chunk] = jnp.concatenate([lower, lower], axis=1)
        if mask_t is not None:
            upper = (same & (row <= col)).astype(F32).astype(BF16)
            mask_t[chunk] = jnp.concatenate([upper, upper], axis=1)


def qkv_kernel(second, where, own, *rest):
    if second:
        came, gain, bias, cols, w, fq, fk, vv, state, normed, x_out = rest
        copies = []
    else:
        gain, bias, cols, w0, w1, w2, w3, fq, fk, vv, state, w, normed, sems = rest
        copies = start_copies(
            (w0, w1, w2, w3), lambda r: w.at[:, :, r * LANES : (r + 1) * LANES], sems, 0
        )
    total = own.shape[0]

    @row_tiles(total)
    def _(rows):
        x = own[rows, :].astype(F32)
        if second:
            x = jnp.where(where[SECTION] == 0, x, came[rows, :].astype(F32))
            x_out[rows, :] = x.astype(BF16)
        unit, _ = normalise(x)
        normed[rows, :] = (unit * gain[0:1, :] + bias[0:1, :]).astype(BF16)

    for copy in copies:
        copy.wait()

    @row_tiles(total, 256)
    def _(rows):
        block = normed[rows, :]
        query = nn(block, w[0])
        fq[rows, :] = jnp.where(query > 0, query + 1.0, jnp.exp(jnp.minimum(query, 0.0))).astype(BF16)
        key = nn(block, w[1])
        key = jnp.where(key > 0, key + 1.0, jnp.exp(jnp.minimum(key, 0.0)))
        fk[rows, :] = (key * cols[rows, PAD : PAD + 1]).astype(BF16)
        vv[rows, :] = nn(block, w[2]).astype(BF16)

    diag = diagonal_blocks()
    for pair in range(state.shape[0]):
        lanes = slice(pair * LANES, (pair + 1) * LANES)
        tail = (fk[:, lanes] * cols[:, TAIL_OUT : TAIL_OUT + 1].astype(BF16)).astype(BF16)
        state[pair] = (diag * tn(tail, side(vv[:, lanes], 1.0))).astype(BF16)


def attention_forward(fq, fk, vv, start, cols, o, inv_den, states, mask):
    diag = diagonal_blocks()

    for pair in range(start.shape[0]):
        lanes = slice(pair * LANES, (pair + 1) * LANES)
        state = start[pair ^ 1].astype(F32)
        for chunk in range(fq.shape[0] // CHUNK):
            span = slice(chunk * CHUNK, (chunk + 1) * CHUNK)
            query, key, value = fq[span, lanes], fk[span, lanes], vv[span, lanes]
            carried = cols[span, CARRIED : CARRIED + 1]
            tail = cols[span, TAIL : TAIL + 1].astype(BF16)
            state_low = state.astype(BF16)
            if states is not None:
                states[pair, chunk] = state_low
            scores = nt(query, split_pair(key)).astype(BF16) * mask[chunk]
            ones = split_pair(jnp.ones_like(value))
            values = jnp.concatenate([split_pair(value), ones], axis=1)
            both = nn(scores, values) + carried * nn(query, state_low)
            inverse = 1.0 / (both[:, LANES:] + 1.0)
            o[span, lanes] = (both[:, :LANES] * inverse).astype(BF16)
            if inv_den is not None:
                inv_den[span, lanes] = inverse
            keep = carried[CHUNK - 1 : CHUNK, :]
            state = keep * state + diag * tn(key * tail, side(value, 1.0))


def out_and_norm(o, x, out_w, gain, bias, mid, normed_two):
    @row_tiles(o.shape[0], 256)
    def _(rows):
        mid[rows, :] = x[rows, :].astype(F32) + nn(o[rows, :], out_w[...])

    @row_tiles(o.shape[0])
    def _(rows):
        unit, _ = normalise(mid[rows, :])
        normed_two[rows, :] = (unit * gain[1:2, :] + bias[1:2, :]).astype(BF16)


def gelu_parts(up, with_slope):
    square = up * up
    inner = jnp.tanh(GELU_C * up * (1.0 + GELU_A * square))
    half = 0.5 * (1.0 + inner)
    if not with_slope:
        return up * half, None
    slope = half + up * (0.5 * GELU_C) * (1.0 - inner * inner) * (1.0 + 3.0 * GELU_A * square)
    return up * half, slope


def attention_kernel(
    fq, fk, vv, start, cols, seg, x, gain, bias, w0, w1, w2, w3, mid, normed_two, w, mask, o, sems
):
    copies = start_copies(
        (w0, w1, w2, w3), lambda r: w.at[r * LANES : (r + 1) * LANES, :], sems, 0
    )
    chunk_masks(cols, seg, mask, None)
    attention_forward(fq, fk, vv, start, cols, o, None, None, mask)
    for copy in copies:
        copy.wait()
    out_and_norm(o, x, w, gain, bias, mid, normed_two)


def up_kernel(normed_two, w0, w1, w2, w3, active):
    width = w0.shape[1]
    for r, w in enumerate((w0, w1, w2, w3)):

        @row_tiles(normed_two.shape[0], 256)
        def _(rows, r=r, w=w):
            up = nn(normed_two[rows, :], w[...])
            active[rows, r * width : (r + 1) * width] = gelu_parts(up, False)[0].astype(BF16)


def down_kernel(mid, active, w0, w1, w2, w3, y):
    width = w0.shape[1]

    @row_tiles(mid.shape[0], 256)
    def _(rows):
        total = mid[rows, :]
        for r, w in enumerate((w0, w1, w2, w3)):
            total = total + nt(active[rows, r * width : (r + 1) * width], w[...])
        y[rows, :] = total.astype(BF16)


def block_kernel(
    fq, fk, vv, start, cols, seg, x, gain, bias, out_w, u0, u1, u2, u3, d0, d1, d2, d3,
    y, mid, o, o_send, inv_den, states, keep, send, slope, normed_two, mask, mask_t,
):
    chunk_masks(cols, seg, mask, mask_t)
    attention_forward(fq, fk, vv, start, cols, o, inv_den, states, mask)
    for slot, r in enumerate((1, 3)):
        o_send[:, slot * LANES : (slot + 1) * LANES] = o[:, r * LANES : (r + 1) * LANES]
    out_and_norm(o, x, out_w, gain, bias, mid, normed_two)
    up_w, down_w = (u0, u1, u2, u3), (d0, d1, d2, d3)
    width = u0.shape[1]

    @row_tiles(x.shape[0], 256)
    def _(rows):
        total = mid[rows, :]
        for r in range(4):
            units = slice(r * width, (r + 1) * width)
            value, steep = gelu_parts(nn(normed_two[rows, :], up_w[r][...]), True)
            value = value.astype(BF16)
            half = slice(r // 2 * width, (r // 2 + 1) * width)
            (send if r % 2 else keep)[rows, half] = value
            slope[rows, units] = steep.astype(BF16)
            total = total + nt(value, down_w[r][...])
        y[rows, :] = total.astype(BF16)


def ffn_rows(rows, gy, slope, up_w, down_w, save):
    width = up_w[0].shape[1]
    dffn = gy[rows, :].astype(BF16)
    grad = jnp.zeros(dffn.shape, F32)
    for r in range(4):
        units = slice(r * width, (r + 1) * width)
        dup = (slope[rows, units].astype(F32) * nn(dffn, down_w[r][...])).astype(BF16)
        if save is not None:
            half = slice(r // 2 * width, (r // 2 + 1) * width)
            save[r % 2][rows, half] = dup
        grad = grad + nt(dup, up_w[r][...])
    return grad


def ffn_back_kernel(second, where, own_g, *rest):
    if second:
        came, rest = rest[0], rest[1:]
    slope, mid, o, inv_den, fq, cols, gain, out_w, *rest = rest
    up_w, down_w = rest[0:4], rest[4:8]
    grad_mid, dnum, dden, grad_state, dattn, *rest = rest[8:]
    gy, save, sums = own_g, None, None
    if second:
        *save, sums, gy = rest

        @row_tiles(gy.shape[0])
        def _(rows):
            gy[rows, :] = jnp.where(
                where[SECTION] == 1, own_g[rows, :], came[rows, :].astype(F32)
            )

    @row_tiles(gy.shape[0], 256)
    def _(rows):
        grad_mid[rows, :] = ffn_rows(rows, gy, slope, up_w, down_w, save)

    mid_back(
        gy, mid, o, inv_den, fq, cols, gain, out_w, grad_mid, dnum, dden, grad_state, dattn, sums
    )


def mid_back(
    gy, mid, o, inv_den, fq, cols, gain, out_w, grad_mid, dnum, dden, grad_state, dattn, sums
):
    total = gy.shape[0]
    if sums is not None:
        sums[...] = jnp.zeros_like(sums)

    @row_tiles(total)
    def _(rows):
        unit, scale = normalise(mid[rows, :])
        grad = grad_mid[rows, :]
        if sums is not None:
            sums[0:1, :] += jnp.sum(grad * unit, axis=0, keepdims=True)
            sums[1:2, :] += jnp.sum(grad, axis=0, keepdims=True)
        grad = gy[rows, :] + norm_backward(grad, unit, scale, gain[1:2, :])
        grad_mid[rows, :] = grad
        dattn[rows, :] = grad.astype(BF16)

    row_a = lax.broadcasted_iota(jnp.int32, (LANES, LANES), 0) < E
    spread = (row_a == first_head((LANES, LANES))).astype(BF16)
    use_low = lax.broadcasted_iota(jnp.int32, (256, LANES), 1) % E >= E // 2

    @row_tiles(total, 256)
    def _(rows):
        grad_heads = nt(dattn[rows, :], out_w[...])
        scaled = grad_heads * inv_den[rows, :]
        dnum[rows, :] = scaled.astype(BF16)
        product = -scaled * o[rows, :].astype(F32)
        for pair in range(grad_state.shape[0]):
            lanes = slice(pair * LANES, (pair + 1) * LANES)
            part = product[:, lanes]
            high = part.astype(BF16)
            low = (part - high.astype(F32)).astype(BF16)
            whole = nn(high, spread) + nn(low, spread)
            high = whole.astype(BF16)
            low = (whole - high.astype(F32)).astype(BF16)
            dden[rows, lanes] = jnp.where(use_low, low, high)

    diag = diagonal_blocks()
    carry_in = cols[:, CARRY_IN : CARRY_IN + 1].astype(BF16)
    for pair in range(grad_state.shape[0]):
        lanes = slice(pair * LANES, (pair + 1) * LANES)
        both = jnp.concatenate([dnum[:, lanes], dden[:, lanes]], axis=1)
        grad_state[pair] = (diag * tn(fq[:, lanes] * carry_in, both)).astype(BF16)


def attention_back_kernel(
    with_weights, fq, fk, vv, dnum, dden, states, end, cols, mask, mask_t, x, grad_mid, gain, w, *rest
):
    if with_weights:
        sums_two, grad_x, keep, send, sums, *rest = rest
    else:
        grad_x, *rest = rest
    acc, dproj = rest
    diag = diagonal_blocks()
    lane = lax.broadcasted_iota(jnp.int32, (1, PAIR), 1)
    share = jnp.where(lane < LANES, 1.0, SPLIT)

    for pair in range(end.shape[0]):
        lanes = slice(pair * LANES, (pair + 1) * LANES)
        grad_state = end[pair ^ 1].astype(F32)
        for chunk in reversed(range(fq.shape[0] // CHUNK)):
            span = slice(chunk * CHUNK, (chunk + 1) * CHUNK)
            query, key, value = fq[span, lanes], fk[span, lanes], vv[span, lanes]
            grad_n, grad_d = dnum[span, lanes], dden[span, lanes]
            carried = cols[span, CARRIED : CARRIED + 1]
            tail = cols[span, TAIL : TAIL + 1]
            stays = carried[CHUNK - 1 : CHUNK, :]
            query_two = split_pair(query)
            grad_n_two = split_pair(grad_n)
            both = jnp.concatenate([grad_n, grad_d], axis=1)
            both_two = jnp.concatenate([grad_n_two, split_pair(grad_d)], axis=1)
            share_two = split_pair(jnp.full(value.shape, SPLIT, BF16))
            values_two = jnp.concatenate([split_pair(value), share_two], axis=1)
            values = side(value, SPLIT)
            scores_t = nt(key, query_two).astype(BF16) * mask_t[chunk]
            dscores = nt(both, values_two).astype(BF16) * mask[chunk]
            dscores_t = nt(values, both_two).astype(BF16) * mask_t[chunk]
            state = (states[pair, chunk].astype(F32) * share).astype(BF16)
            grad_low = grad_state.astype(BF16)
            dfq = nn(dscores, split_pair(key)) + carried * nt(both, state)
            dfk = nn(dscores_t, query_two) + tail * nt(values, grad_low)
            dvv = nn(scores_t, grad_n_two) + tail * nn(key, grad_low[:, :LANES])
            dproj[0, span, lanes] = (jnp.minimum(query.astype(F32), 1.0) * dfq).astype(BF16)
            dproj[1, span, lanes] = (jnp.minimum(key.astype(F32), 1.0) * dfk).astype(BF16)
            dproj[2, span, lanes] = dvv.astype(BF16)
            moved = diag * tn(query * carried.astype(BF16), both)
            grad_state = stays * grad_state + moved

    @row_tiles(x.shape[0], 256)
    def _(rows):
        acc[rows, :] = (
            nt(dproj[0, rows, :], w[0]) + nt(dproj[1, rows, :], w[1]) + nt(dproj[2, rows, :], w[2])
        )

    if with_weights:
        for r in range(4):
            half = slice(r // 2 * LANES, (r // 2 + 1) * LANES)
            (send if r % 2 else keep)[:, :, half] = dproj[:, :, r * LANES : (r + 1) * LANES]
        sums[...] = jnp.zeros_like(sums)
        sums[1:2, :] = sums_two[0:1, :]
        sums[3:4, :] = sums_two[1:2, :]

    @row_tiles(x.shape[0])
    def _(rows):
        unit, scale = normalise(x[rows, :].astype(F32))
        grad = acc[rows, :]
        if with_weights:
            sums[0:1, :] += jnp.sum(grad * unit, axis=0, keepdims=True)
            sums[2:3, :] += jnp.sum(grad, axis=0, keepdims=True)
        grad = grad_mid[rows, :] + norm_backward(grad, unit, scale, gain[0:1, :])
        grad_x[rows, :] = grad.astype(BF16)


def down_grad_kernel(where, own_g, other_g, came, came_two, own, other, keep, send, turned):
    total = own_g.shape[0]
    for n, (mine, arrived) in enumerate(((own_g, came), (other_g, came_two))):
        whole = jnp.where(where[SECTION] == 1, mine[...], arrived[...].astype(F32))
        turned[:, n * total : (n + 1) * total] = whole.astype(BF16).T
    width = keep.shape[1]
    for r, place in enumerate((keep, send)):
        cols = slice(r * width, (r + 1) * width)
        sum_own = nn(turned[:, :total], own[:, cols])
        place[...] = (sum_own + nn(turned[:, total:], other[:, cols])).astype(BF16)


def up_grad_kernel(normed_own, normed_other, own, other, keep, send, turned):
    total = normed_own.shape[0]
    turned[:, :total] = normed_own[...].T
    turned[:, total:] = normed_other[...].T
    width = keep.shape[1]
    for r, place in enumerate((keep, send)):
        cols = slice(r * width, (r + 1) * width)
        sum_own = nn(turned[:, :total], own[:, cols])
        place[...] = (sum_own + nn(turned[:, total:], other[:, cols])).astype(BF16)


def late_grad_kernel(
    normed_own, normed_other, own, other, o_own, o_other, dattn_own, dattn_other,
    sums_own, sums_other, keep, send, turned,
):
    total, width = normed_own.shape
    base = 3 * width
    last = base + width
    places = (keep, send)
    turned[:, :total] = normed_own[...].T
    turned[:, total:] = normed_other[...].T
    for c in range(3):
        whole = nn(turned[:, :total], own[c]) + nn(turned[:, total:], other[c])
        for r, place in enumerate(places):
            cols = slice(r * LANES, (r + 1) * LANES)
            place[c * width : (c + 1) * width, :] = whole[:, cols].astype(BF16)
    for r, place in enumerate(places):
        here = o_own[:, 2 * r * LANES : (2 * r + 1) * LANES].T
        there = o_other[:, r * LANES : (r + 1) * LANES].T
        whole = (nn(here, dattn_own[...]) + nn(there, dattn_other[...])).astype(BF16)
        for n in range(width // LANES):
            to = base + n * LANES
            place[to : to + LANES, :] = whole[:, n * LANES : (n + 1) * LANES]
    four = sums_own[0:4, :] + sums_other[0:4, :]
    small = jnp.concatenate(
        [four[v : v + 1, n * LANES : (n + 1) * LANES] for v in range(4) for n in range(width // LANES)],
        axis=0,
    ).astype(BF16)
    for place in places:
        place[last : last + small.shape[0], :] = small
        left = place.shape[0] - last - small.shape[0]
        place[last + small.shape[0] :, :] = jnp.zeros((left, LANES), BF16)


def unpack_late(source, qkv, out, gains, biases):
    width = out.shape[1]
    base = 3 * width
    last = base + width
    pairs = width // LANES
    for c in range(3):
        qkv[c] = source[c * width : (c + 1) * width, :].astype(F32)
    for n in range(pairs):
        cols = slice(n * LANES, (n + 1) * LANES)
        out[:, cols] = source[base + n * LANES : base + (n + 1) * LANES, :].astype(F32)
        for v, place in enumerate((gains, gains, biases, biases)):
            row = last + v * pairs + n
            place[v % 2 : v % 2 + 1, cols] = source[row : row + 1, :].astype(F32)


def join_late_kernel(where, own, came, qkv, out, gains, biases, whole):
    whole_kernel(where, own, came, whole)
    unpack_late(whole, qkv, out, gains, biases)


def unpack_late_kernel(source, qkv, out, gains, biases, whole):
    whole[...] = source[...].astype(F32)
    unpack_late(whole, qkv, out, gains, biases)


def my_half(where):
    depth = where[DEPTH]
    return (depth ^ (depth >> 1)) & 1


def rows_at(index, size):
    return pl.ds(pl.multiple_of(index * size, 16), size)


def halve_kernel(where, keep, came, stays, goes):
    mine = my_half(where)
    size = stays.shape[0]
    for index, out in ((mine, stays), (1 - mine, goes)):
        rows = rows_at(index, size)
        out[...] = (keep[rows, :].astype(F32) + came[rows, :].astype(F32)).astype(out.dtype)


def sum_kernel(keep, came, out):
    out[...] = (keep[...].astype(F32) + came[...].astype(F32)).astype(BF16)


def whole_kernel(where, own, came, out):
    mine = my_half(where)
    size = own.shape[0]
    out[rows_at(mine, size), :] = own[...].astype(F32)
    out[rows_at(1 - mine, size), :] = came[...].astype(F32)


def finish_kernel(with_rms, where, p0, p1, p2, p3, out, *rms):
    total, width = p0.shape
    for r, part in enumerate((p0, p1, p2, p3)):
        begin = where[PLACE] ^ r

        @pl.loop(0, total // LANES, unroll=True)
        def _(tile, part=part, begin=begin):
            block = part[pl.ds(pl.multiple_of(tile * LANES, LANES), LANES), :].astype(F32)
            to = begin * (total // LANES) + tile
            out[pl.ds(pl.multiple_of(to * LANES, LANES), LANES), :] = block
            if with_rms:
                square = block * block
                high = square.astype(BF16)
                low = (square - high.astype(F32)).astype(BF16)
                ones = jnp.ones((width, LANES), BF16)
                mean = (nn(high, ones) + nn(low, ones)) * (1.0 / width)
                row = lax.broadcasted_iota(jnp.int32, (LANES, LANES), 0)
                col = lax.broadcasted_iota(jnp.int32, (LANES, LANES), 1)
                mean = jnp.sum(jnp.where(row == col, mean, 0.0), axis=0, keepdims=True)
                rms[0][pl.ds(to, 1), :] = jnp.sqrt(mean + 1e-06)


IN_VMEM = pl.BlockSpec(memory_space=pltpu.VMEM)
IN_SMEM = pl.BlockSpec(memory_space=pltpu.SMEM)
ANYWHERE = pl.BlockSpec(memory_space=pl.ANY)


def call(kernel, operands, outputs, scratch, name, us, far=()):
    near = [jax.ShapeDtypeStruct(shape, dtype) for shape, dtype in outputs]
    return pl.pallas_call(
        kernel,
        out_shape=near,
        in_specs=[IN_SMEM if v.dtype == jnp.int32 else IN_VMEM for v in operands]
        + [ANYWHERE] * len(far),
        out_specs=[IN_VMEM] * len(near),
        scratch_shapes=scratch,
        compiler_params=pltpu.CompilerParams(vmem_limit_bytes=VMEM_LIMIT),
        cost_estimate=pl.CostEstimate(
            flops=int(us * 1.1e9), bytes_accessed=0, transcendentals=0
        ),
        name=name,
    )(*operands, *far)


def across(block, distance, axis="head"):
    size = lax.axis_size(axis)
    return lax.ppermute(block, axis, [(i, i ^ distance) for i in range(size)])


def spread(block, far):
    return (block, across(block, 1), far, across(far, 1))


def after(value, *others):
    return lax.optimization_barrier((value, *others))[0]


def sum_over_dp(keep, came, where, name, join):
    rows, width = keep.shape
    if lax.axis_size("dp") != 4:
        total = (keep.astype(F32) + came.astype(F32)).astype(BF16)
        return join(lax.psum(total, "dp"))
    half = (rows // 2, width)
    stays, goes = call(
        halve_kernel, (where, keep, came), [(half, F32), (half, BF16)], [], "halve_" + name, 0.8
    )
    (own,) = call(
        sum_kernel, (stays, across(goes, 1, "dp")), [(half, BF16)], [], "sum_near_" + name, 0.7
    )
    (own,) = call(
        sum_kernel, (own, across(own, 3, "dp")), [(half, BF16)], [], "sum_far_" + name, 0.7
    )
    return join(where, own, across(own, 1, "dp"))


def finish(where, own, far, with_rms, name):
    rows, width = own.shape[0] * 4, own.shape[1]
    outputs = [((rows, width), F32)] + [((rows // LANES, LANES), F32)] * with_rms
    return call(
        functools.partial(finish_kernel, with_rms),
        (where, own, across(own, 1), far, across(far, 1)), outputs, [], name, 3.0,
    )


def token_table(segment_start, pad_mask, place, tokens, parts):
    row_count = segment_start.shape[0] // SEQ
    ids = jnp.cumsum(segment_start.reshape(row_count, SEQ), axis=1).reshape(-1)
    begin = place * tokens
    own = lax.dynamic_slice(ids, (begin,), (tokens,))
    before = lax.dynamic_slice(ids, (jnp.maximum(begin - 1, 0),), (1,))
    before = jnp.where(place % parts == 0, jnp.full_like(before, -1), before)
    last = own.reshape(-1, CHUNK)[:, -1]
    previous = jnp.concatenate([before, last[:-1]])
    pad = lax.dynamic_slice(pad_mask, (begin,), (tokens,))
    columns = [
        pad,
        own,
        own == before,
        own == last[-1:],
        own == jnp.repeat(previous, CHUNK),
        own == jnp.repeat(last, CHUNK),
    ]
    columns = jnp.stack([c.astype(F32) for c in columns], axis=1)
    rows = jnp.broadcast_to(own.astype(F32)[None], (8, tokens))
    return columns, rows


def local(
    block_input, cotangent, segment_start, pad_mask, qkv_weight, out_weight, up_weight,
    down_weight, norm_gain, norm_bias,
):
    heads = lax.axis_size("head")
    row_count = block_input.shape[0] // SEQ
    parts = heads // row_count
    assert heads == 4 and parts == 2
    tokens = block_input.shape[0] // heads
    width = block_input.shape[1]
    units = up_weight.shape[-1] * heads
    pairs = width // LANES
    chunks = tokens // CHUNK
    section = lax.axis_index("section")
    place = lax.axis_index("head")

    gain, bias = norm_gain[0], norm_bias[0]
    far_out = across(out_weight[0], 2)
    far_up = across(up_weight[0], 2)
    far_down = across(down_weight[0], 2)

    cols, seg = token_table(segment_start, pad_mask, place, tokens, parts)
    own_x = lax.dynamic_slice(block_input, (place * tokens, 0), (tokens, width))

    wide = (tokens, width)
    state_shape = (pairs, LANES, PAIR)
    dma = pltpu.SemaphoreType.DMA
    mask_shape = ((chunks, CHUNK, PAIR), BF16)
    mask_mem = pltpu.VMEM(*mask_shape)
    row_mem = pltpu.VMEM(wide, BF16)

    own_g = lax.dynamic_slice(cotangent, (place * tokens, 0), (tokens, width))
    other_g = lax.dynamic_slice(cotangent, ((place ^ 1) * tokens, 0), (tokens, width))
    where = jnp.stack([section, place, lax.axis_index("dp")]).astype(jnp.int32)
    turned_mem = pltpu.VMEM((width, 2 * tokens), BF16)
    grad_mem = pltpu.VMEM(wide, F32)
    half = (tokens, units // 2)
    features = [(wide, BF16)] * 3 + [(state_shape, BF16)]

    fq, fk, vv, state, qkv = call(
        functools.partial(qkv_kernel, False),
        (where, after(own_x, own_g, other_g, seg), gain, bias, cols),
        features + [((3, width, width), BF16)],
        [row_mem, dma((4,))], "qkv_first", 4.0, far=spread(qkv_weight[0], across(qkv_weight[0], 2)),
    )
    start = across(state, 1)
    mid, normed_two, out_w = call(
        attention_kernel, (fq, fk, vv, start, cols, seg, own_x, gain, bias),
        [(wide, F32), (wide, BF16), ((width, width), BF16)],
        [mask_mem, row_mem, dma((4,))], "attention_first", 5.5,
        far=spread(out_weight[0], after(far_out, fq)),
    )
    up_w = spread(up_weight[0], after(far_up, fq))
    (active,) = call(
        up_kernel, (normed_two, *up_w), [((tokens, units), BF16)], [], "up_first", 3.2
    )
    down_w = spread(down_weight[0], after(far_down, active))
    (y,) = call(down_kernel, (mid, active, *down_w), [(wide, BF16)], [], "down_first", 2.8)
    came = across(y, 1, "section")

    fq, fk, vv, state, normed, x = call(
        functools.partial(qkv_kernel, True), (where, own_x, came, gain, bias, cols, qkv),
        features + [(wide, BF16)] * 2, [], "qkv_second", 3.5,
    )
    start = across(state, 1)
    y, mid, o, o_send, inv_den, states, active, active_send, slope, normed_two, *masks = call(
        block_kernel, (fq, fk, vv, start, cols, seg, x, gain, bias, out_w, *up_w, *down_w),
        [
            (wide, BF16), (wide, F32), (wide, BF16), ((tokens, width // 2), BF16), (wide, F32),
            ((pairs, chunks, LANES, PAIR), BF16), (half, BF16), (half, BF16),
            ((tokens, units), BF16), (wide, BF16), mask_shape, mask_shape,
        ],
        [], "block_second", 10.0,
    )
    far_y = across(y, 2)
    active_two = across(active_send, 1)
    normed_other = across(normed, 1)
    normed_two_other = across(normed_two, 1)
    o_other = across(o_send, 1)

    def attention_back(sums, grad_mid, dnum, dden, end, name):
        third = ((3, tokens, width // 2), BF16)
        extra = [third, third, ((8, width), F32)] if sums else []
        return call(
            functools.partial(attention_back_kernel, bool(sums)),
            (fq, fk, vv, dnum, dden, states, end, cols, *masks, x, grad_mid, gain, qkv, *sums),
            [(wide, BF16)] + extra,
            [grad_mem, pltpu.VMEM((3, *wide), BF16)], name, (LOW if sums else 1.0) * 7.5,
        )

    back_shapes = [(wide, F32), (wide, BF16), (wide, BF16), (state_shape, BF16)]
    back_operands = (slope, mid, o, inv_den, fq, cols, gain, out_w, *up_w, *down_w)
    grad_mid, dnum, dden, moved = call(
        functools.partial(ffn_back_kernel, False), (where, own_g, *back_operands),
        back_shapes, [row_mem], "ffn_back_first", 4.2,
    )
    (grad_x,) = attention_back((), grad_mid, dnum, dden, across(moved, 1), "attention_back_first")
    came = across(grad_x, 1, "section")
    came = after(came, far_y)

    share = (width, units // 4)
    keep, send = call(
        down_grad_kernel, (where, own_g, other_g, came, across(came, 1), active, active_two),
        [(share, BF16)] * 2, [turned_mem], "down_grad", LOW * 2.2,
    )
    down_keep, down_far = keep, across(send, 2)
    grad_mid, dnum, dden, moved, dattn, dup, dup_send, sums_two = call(
        functools.partial(ffn_back_kernel, True),
        (where, own_g, after(came, send), *back_operands),
        back_shapes + [(wide, BF16), (half, BF16), (half, BF16), ((2, width), F32)],
        [grad_mem], "ffn_back_second", LOW * 5.0,
    )
    dup_other = across(dup_send, 1)
    end = across(moved, 1)
    dattn_other = across(dattn, 1)
    grad_x, dproj, dproj_send, sums = attention_back(
        (sums_two,), grad_mid, dnum, dden, end, "attention_back_second"
    )
    dproj_other = across(dproj_send, 1)
    keep, send = call(
        up_grad_kernel,
        (normed_two, normed_two_other, dup, after(dup_other, grad_x, down_far)),
        [(share, BF16)] * 2, [turned_mem], "up_grad", 1.3,
    )
    up_keep, up_far = keep, across(send, 2)
    dproj_other = after(dproj_other, send)
    late = (4 * width + 64, LANES)
    keep, send = call(
        late_grad_kernel,
        (
            normed, normed_other, dproj, dproj_other, o, o_other, dattn, dattn_other,
            sums, across(sums, 1),
        ),
        [(late, BF16)] * 2, [turned_mem], "late_grad", 1.3,
    )
    late_far = across(send, 2)
    def join_plain(*parts):
        if len(parts) == 1:
            return parts[0].astype(F32)
        return call(whole_kernel, parts, [(share, F32)], [], "whole", 1.5)[0]

    def join_late(*parts):
        results = [
            ((3, width, LANES), F32), ((LANES, width), F32), ((2, width), F32), ((2, width), F32)
        ]
        kernel = unpack_late_kernel if len(parts) == 1 else join_late_kernel
        return call(kernel, parts, results, [pltpu.VMEM(late, F32)], "join_late", 1.5)

    down_total = sum_over_dp(down_keep, after(down_far, send), where, "down", join_plain)
    up_total = sum_over_dp(up_keep, up_far, where, "up", join_plain)
    qkv_total, out_total, gain_total, bias_total = sum_over_dp(
        keep, late_far, where, "late", join_late
    )
    activations, token_rms = finish(where, after(y, up_total), after(far_y, up_total), True, "activations")
    own = after(grad_x, send)
    (input_grad,) = finish(where, own, across(own, 2), False, "input_grad")
    return (
        activations[None], input_grad[None], token_rms.reshape(1, -1), qkv_total[None],
        out_total[None], up_total[None], down_total[None], gain_total[None], bias_total[None],
    )


def solution(mesh):
    placed = (
        P("dp", None),
        P("dp", None),
        P("dp"),
        P("dp"),
        P("section", None, None, "head"),
        P("section", "head", None),
        P("section", None, "head"),
        P("section", None, "head"),
        P("section", None, None),
        P("section", None, None),
    )
    return jax.shard_map(
        local,
        mesh=mesh,
        in_specs=placed,
        out_specs=(
            P("section", "dp", None),
            P("section", "dp", None),
            P("section", "dp"),
            P("section", None, None, "head"),
            P("section", "head", None),
            P("section", None, "head"),
            P("section", None, "head"),
            P("section", None, None),
            P("section", None, None),
        ),
        check_vma=False,
    )
```

```python
import functools

import jax
import jax.numpy as jnp
from jax import lax
from jax.experimental import pallas as pl
from jax.experimental.pallas import tpu as pltpu
from jax.sharding import PartitionSpec as P

E = 64
SEQ = 1024
LANES = 128
PAIR = 2 * LANES
CHUNK = 256
EPS = 1e-05
F32 = jnp.float32
BF16 = jnp.bfloat16
ROWS = 128
GELU_C = 0.7978845608028654
GELU_A = 0.044715
SPLIT = 1.0 / 32.0
LOW = 0.02
VMEM_LIMIT = 16 * 1024 * 1024

SECTION, PLACE, DEPTH = range(3)

PAD, SEG, CARRY_IN, TAIL_OUT, CARRIED, TAIL = range(6)


def nn(a, b):
    return jnp.dot(a, b, preferred_element_type=F32)


def nt(a, b):
    return lax.dot_general(a, b, (((1,), (1,)), ((), ())), preferred_element_type=F32)


def tn(a, b):
    return lax.dot_general(a, b, (((0,), (0,)), ((), ())), preferred_element_type=F32)


def first_head(shape):
    return lax.broadcasted_iota(jnp.int32, shape, len(shape) - 1) % LANES < E


def diagonal_blocks():
    row = lax.broadcasted_iota(jnp.int32, (LANES, PAIR), 0) < E
    return (row == first_head((LANES, PAIR))).astype(F32)


def split_pair(block):
    in_a = first_head(block.shape)
    zero = jnp.zeros_like(block)
    return jnp.concatenate([jnp.where(in_a, block, zero), jnp.where(in_a, zero, block)], axis=0)


def side(block, fill):
    return jnp.concatenate([block, jnp.full(block.shape, fill, block.dtype)], axis=1)


def normalise(values):
    centre = jnp.mean(values, axis=-1, keepdims=True)
    shifted = values - centre
    scale = lax.rsqrt(jnp.mean(shifted * shifted, axis=-1, keepdims=True) + EPS)
    return shifted * scale, scale


def norm_backward(grad, unit, scale, gain):
    grad_unit = grad * gain
    mean_grad = jnp.mean(grad_unit, axis=-1, keepdims=True)
    mean_dot = jnp.mean(grad_unit * unit, axis=-1, keepdims=True)
    return scale * (grad_unit - mean_grad - unit * mean_dot)


def row_tiles(total, step=ROWS):
    def decorate(body):
        pl.loop(0, total // step, unroll=True)(
            lambda index: body(pl.ds(pl.multiple_of(index * step, step), step))
        )

    return decorate


def start_copies(parts, place, sems, base):
    copies = [
        pltpu.make_async_copy(part, place(r), sems.at[base + r]) for r, part in enumerate(parts)
    ]
    for copy in copies:
        copy.start()
    return copies


def chunk_masks(cols_ref, seg_ref, mask, mask_t):
    row = lax.broadcasted_iota(jnp.int32, (CHUNK, CHUNK), 0)
    col = lax.broadcasted_iota(jnp.int32, (CHUNK, CHUNK), 1)
    for chunk in range(cols_ref.shape[0] // CHUNK):
        span = slice(chunk * CHUNK, (chunk + 1) * CHUNK)
        same = cols_ref[span, SEG : SEG + 1] == seg_ref[0:1, span]
        if mask is not None:
            lower = (same & (col <= row)).astype(F32).astype(BF16)
            mask[chunk] = jnp.concatenate([lower, lower], axis=1)
        if mask_t is not None:
            upper = (same & (row <= col)).astype(F32).astype(BF16)
            mask_t[chunk] = jnp.concatenate([upper, upper], axis=1)


def qkv_kernel(second, where, own, *rest):
    if second:
        came, gain, bias, cols, w, fq, fk, vv, state, normed, x_out = rest
        copies = []
    else:
        gain, bias, cols, w0, w1, w2, w3, fq, fk, vv, state, w, normed, sems = rest
        copies = start_copies(
            (w0, w1, w2, w3), lambda r: w.at[:, :, r * LANES : (r + 1) * LANES], sems, 0
        )
    total = own.shape[0]

    @row_tiles(total)
    def _(rows):
        x = own[rows, :].astype(F32)
        if second:
            x = jnp.where(where[SECTION] == 0, x, came[rows, :].astype(F32))
            x_out[rows, :] = x.astype(BF16)
        unit, _ = normalise(x)
        normed[rows, :] = (unit * gain[0:1, :] + bias[0:1, :]).astype(BF16)

    for copy in copies:
        copy.wait()

    @row_tiles(total, 256)
    def _(rows):
        block = normed[rows, :]
        query = nn(block, w[0])
        fq[rows, :] = jnp.where(query > 0, query + 1.0, jnp.exp(jnp.minimum(query, 0.0))).astype(BF16)
        key = nn(block, w[1])
        key = jnp.where(key > 0, key + 1.0, jnp.exp(jnp.minimum(key, 0.0)))
        fk[rows, :] = (key * cols[rows, PAD : PAD + 1]).astype(BF16)
        vv[rows, :] = nn(block, w[2]).astype(BF16)

    diag = diagonal_blocks()
    for pair in range(state.shape[0]):
        lanes = slice(pair * LANES, (pair + 1) * LANES)
        tail = (fk[:, lanes] * cols[:, TAIL_OUT : TAIL_OUT + 1].astype(BF16)).astype(BF16)
        state[pair] = (diag * tn(tail, side(vv[:, lanes], 1.0))).astype(BF16)


def attention_forward(fq, fk, vv, start, cols, o, inv_den, states, mask):
    diag = diagonal_blocks()

    for pair in range(start.shape[0]):
        lanes = slice(pair * LANES, (pair + 1) * LANES)
        state = start[pair ^ 1].astype(F32)
        for chunk in range(fq.shape[0] // CHUNK):
            span = slice(chunk * CHUNK, (chunk + 1) * CHUNK)
            query, key, value = fq[span, lanes], fk[span, lanes], vv[span, lanes]
            carried = cols[span, CARRIED : CARRIED + 1]
            tail = cols[span, TAIL : TAIL + 1].astype(BF16)
            state_low = state.astype(BF16)
            if states is not None:
                states[pair, chunk] = state_low
            scores = nt(query, split_pair(key)).astype(BF16) * mask[chunk]
            ones = split_pair(jnp.ones_like(value))
            values = jnp.concatenate([split_pair(value), ones], axis=1)
            both = nn(scores, values) + carried * nn(query, state_low)
            inverse = 1.0 / (both[:, LANES:] + 1.0)
            o[span, lanes] = (both[:, :LANES] * inverse).astype(BF16)
            if inv_den is not None:
                inv_den[span, lanes] = inverse
            keep = carried[CHUNK - 1 : CHUNK, :]
            state = keep * state + diag * tn(key * tail, side(value, 1.0))


def out_and_norm(o, x, out_w, gain, bias, mid, normed_two):
    @row_tiles(o.shape[0], 256)
    def _(rows):
        mid[rows, :] = x[rows, :].astype(F32) + nn(o[rows, :], out_w[...])

    @row_tiles(o.shape[0])
    def _(rows):
        unit, _ = normalise(mid[rows, :])
        normed_two[rows, :] = (unit * gain[1:2, :] + bias[1:2, :]).astype(BF16)


def gelu_parts(up, with_slope):
    half = 0.5 + 0.5 * jnp.tanh(up * (GELU_C + GELU_C * GELU_A * (up * up)))
    half, up = half.astype(BF16), up.astype(BF16)
    value = up * half
    if not with_slope:
        return value, None
    slope = 2 * GELU_C + 6 * GELU_C * GELU_A * (up * up)
    return value, half + value * (1.0 - half) * slope


def attention_kernel(
    fq, fk, vv, start, cols, seg, x, gain, bias, w0, w1, w2, w3, mid, normed_two, w, mask, o, sems
):
    copies = start_copies(
        (w0, w1, w2, w3), lambda r: w.at[r * LANES : (r + 1) * LANES, :], sems, 0
    )
    chunk_masks(cols, seg, mask, None)
    attention_forward(fq, fk, vv, start, cols, o, None, None, mask)
    for copy in copies:
        copy.wait()
    out_and_norm(o, x, w, gain, bias, mid, normed_two)


def up_kernel(normed_two, w0, w1, w2, w3, active):
    width = w0.shape[1]
    for r, w in enumerate((w0, w1, w2, w3)):

        @row_tiles(normed_two.shape[0], 256)
        def _(rows, r=r, w=w):
            up = nn(normed_two[rows, :], w[...])
            active[rows, r * width : (r + 1) * width] = gelu_parts(up, False)[0]


def down_kernel(mid, active, w0, w1, w2, w3, y):
    width = w0.shape[1]

    @row_tiles(mid.shape[0], 256)
    def _(rows):
        total = mid[rows, :]
        for r, w in enumerate((w0, w1, w2, w3)):
            total = total + nt(active[rows, r * width : (r + 1) * width], w[...])
        y[rows, :] = total.astype(BF16)


def block_kernel(
    fq, fk, vv, start, cols, seg, x, gain, bias, out_w, u0, u1, u2, u3, d0, d1, d2, d3,
    y, mid, o, o_send, inv_den, states, keep, send, slope, normed_two, mask, mask_t,
):
    chunk_masks(cols, seg, mask, mask_t)
    attention_forward(fq, fk, vv, start, cols, o, inv_den, states, mask)
    for slot, r in enumerate((1, 3)):
        o_send[:, slot * LANES : (slot + 1) * LANES] = o[:, r * LANES : (r + 1) * LANES]
    out_and_norm(o, x, out_w, gain, bias, mid, normed_two)
    up_w, down_w = (u0, u1, u2, u3), (d0, d1, d2, d3)
    width = u0.shape[1]

    @row_tiles(x.shape[0], 256)
    def _(rows):
        total = mid[rows, :]
        for r in range(4):
            units = slice(r * width, (r + 1) * width)
            value, steep = gelu_parts(nn(normed_two[rows, :], up_w[r][...]), True)
            half = slice(r // 2 * width, (r // 2 + 1) * width)
            (send if r % 2 else keep)[rows, half] = value
            slope[rows, units] = steep
            total = total + nt(value, down_w[r][...])
        y[rows, :] = total.astype(BF16)


def ffn_rows(rows, gy, slope, up_w, down_w, save):
    width = up_w[0].shape[1]
    dffn = gy[rows, :].astype(BF16)
    grad = jnp.zeros(dffn.shape, F32)
    for r in range(4):
        units = slice(r * width, (r + 1) * width)
        dup = slope[rows, units] * nn(dffn, down_w[r][...]).astype(BF16)
        if save is not None:
            half = slice(r // 2 * width, (r // 2 + 1) * width)
            save[r % 2][rows, half] = dup
        grad = grad + nt(dup, up_w[r][...])
    return grad


def ffn_back_kernel(second, where, own_g, *rest):
    if second:
        came, rest = rest[0], rest[1:]
    slope, mid, o, inv_den, fq, cols, gain, out_w, *rest = rest
    up_w, down_w = rest[0:4], rest[4:8]
    grad_mid, dnum, dden, grad_state, dattn, *rest = rest[8:]
    gy, save, sums = own_g, None, None
    if second:
        *save, sums, gy = rest

        @row_tiles(gy.shape[0])
        def _(rows):
            gy[rows, :] = jnp.where(
                where[SECTION] == 1, own_g[rows, :], came[rows, :].astype(F32)
            )

    @row_tiles(gy.shape[0], 256)
    def _(rows):
        grad_mid[rows, :] = ffn_rows(rows, gy, slope, up_w, down_w, save)

    mid_back(
        gy, mid, o, inv_den, fq, cols, gain, out_w, grad_mid, dnum, dden, grad_state, dattn, sums
    )


def mid_back(
    gy, mid, o, inv_den, fq, cols, gain, out_w, grad_mid, dnum, dden, grad_state, dattn, sums
):
    total = gy.shape[0]
    if sums is not None:
        sums[...] = jnp.zeros_like(sums)

    @row_tiles(total)
    def _(rows):
        unit, scale = normalise(mid[rows, :])
        grad = grad_mid[rows, :]
        if sums is not None:
            sums[0:1, :] += jnp.sum(grad * unit, axis=0, keepdims=True)
            sums[1:2, :] += jnp.sum(grad, axis=0, keepdims=True)
        grad = gy[rows, :] + norm_backward(grad, unit, scale, gain[1:2, :])
        grad_mid[rows, :] = grad
        dattn[rows, :] = grad.astype(BF16)

    row_a = lax.broadcasted_iota(jnp.int32, (LANES, LANES), 0) < E
    spread = (row_a == first_head((LANES, LANES))).astype(BF16)
    use_low = lax.broadcasted_iota(jnp.int32, (256, LANES), 1) % E >= E // 2

    @row_tiles(total, 256)
    def _(rows):
        grad_heads = nt(dattn[rows, :], out_w[...])
        scaled = grad_heads * inv_den[rows, :]
        dnum[rows, :] = scaled.astype(BF16)
        product = -scaled * o[rows, :].astype(F32)
        for pair in range(grad_state.shape[0]):
            lanes = slice(pair * LANES, (pair + 1) * LANES)
            part = product[:, lanes]
            high = part.astype(BF16)
            low = (part - high.astype(F32)).astype(BF16)
            whole = nn(high, spread) + nn(low, spread)
            high = whole.astype(BF16)
            low = (whole - high.astype(F32)).astype(BF16)
            dden[rows, lanes] = jnp.where(use_low, low, high)

    diag = diagonal_blocks()
    carry_in = cols[:, CARRY_IN : CARRY_IN + 1].astype(BF16)
    for pair in range(grad_state.shape[0]):
        lanes = slice(pair * LANES, (pair + 1) * LANES)
        both = jnp.concatenate([dnum[:, lanes], dden[:, lanes]], axis=1)
        grad_state[pair] = (diag * tn(fq[:, lanes] * carry_in, both)).astype(BF16)


def attention_back_kernel(
    with_weights, fq, fk, vv, dnum, dden, states, end, cols, mask, mask_t, x, grad_mid, gain, w, *rest
):
    if with_weights:
        sums_two, grad_x, keep, send, sums, *rest = rest
    else:
        grad_x, *rest = rest
    acc, dproj = rest
    diag = diagonal_blocks()
    lane = lax.broadcasted_iota(jnp.int32, (1, PAIR), 1)
    share = jnp.where(lane < LANES, 1.0, SPLIT)

    for pair in range(end.shape[0]):
        lanes = slice(pair * LANES, (pair + 1) * LANES)
        grad_state = end[pair ^ 1].astype(F32)
        for chunk in reversed(range(fq.shape[0] // CHUNK)):
            span = slice(chunk * CHUNK, (chunk + 1) * CHUNK)
            query, key, value = fq[span, lanes], fk[span, lanes], vv[span, lanes]
            grad_n, grad_d = dnum[span, lanes], dden[span, lanes]
            carried = cols[span, CARRIED : CARRIED + 1]
            tail = cols[span, TAIL : TAIL + 1]
            stays = carried[CHUNK - 1 : CHUNK, :]
            query_two = split_pair(query)
            grad_n_two = split_pair(grad_n)
            both = jnp.concatenate([grad_n, grad_d], axis=1)
            both_two = jnp.concatenate([grad_n_two, split_pair(grad_d)], axis=1)
            share_two = split_pair(jnp.full(value.shape, SPLIT, BF16))
            values_two = jnp.concatenate([split_pair(value), share_two], axis=1)
            values = side(value, SPLIT)
            scores_t = nt(key, query_two).astype(BF16) * mask_t[chunk]
            dscores = nt(both, values_two).astype(BF16) * mask[chunk]
            dscores_t = nt(values, both_two).astype(BF16) * mask_t[chunk]
            state = (states[pair, chunk].astype(F32) * share).astype(BF16)
            grad_low = grad_state.astype(BF16)
            dfq = nn(dscores, split_pair(key)) + carried * nt(both, state)
            dfk = nn(dscores_t, query_two) + tail * nt(values, grad_low)
            dvv = nn(scores_t, grad_n_two) + tail * nn(key, grad_low[:, :LANES])
            dproj[0, span, lanes] = (jnp.minimum(query.astype(F32), 1.0) * dfq).astype(BF16)
            dproj[1, span, lanes] = (jnp.minimum(key.astype(F32), 1.0) * dfk).astype(BF16)
            dproj[2, span, lanes] = dvv.astype(BF16)
            moved = diag * tn(query * carried.astype(BF16), both)
            grad_state = stays * grad_state + moved

    @row_tiles(x.shape[0], 256)
    def _(rows):
        acc[rows, :] = (
            nt(dproj[0, rows, :], w[0]) + nt(dproj[1, rows, :], w[1]) + nt(dproj[2, rows, :], w[2])
        )

    if with_weights:
        for r in range(4):
            half = slice(r // 2 * LANES, (r // 2 + 1) * LANES)
            (send if r % 2 else keep)[:, :, half] = dproj[:, :, r * LANES : (r + 1) * LANES]
        sums[...] = jnp.zeros_like(sums)
        sums[1:2, :] = sums_two[0:1, :]
        sums[3:4, :] = sums_two[1:2, :]

    @row_tiles(x.shape[0])
    def _(rows):
        unit, scale = normalise(x[rows, :].astype(F32))
        grad = acc[rows, :]
        if with_weights:
            sums[0:1, :] += jnp.sum(grad * unit, axis=0, keepdims=True)
            sums[2:3, :] += jnp.sum(grad, axis=0, keepdims=True)
        grad = grad_mid[rows, :] + norm_backward(grad, unit, scale, gain[0:1, :])
        grad_x[rows, :] = grad.astype(BF16)


def down_grad_kernel(where, own_g, other_g, came, came_two, own, other, keep, send, turned):
    total = own_g.shape[0]
    for n, (mine, arrived) in enumerate(((own_g, came), (other_g, came_two))):
        whole = jnp.where(where[SECTION] == 1, mine[...], arrived[...].astype(F32))
        turned[:, n * total : (n + 1) * total] = whole.astype(BF16).T
    width = keep.shape[1]
    for r, place in enumerate((keep, send)):
        cols = slice(r * width, (r + 1) * width)
        sum_own = nn(turned[:, :total], own[:, cols])
        place[...] = (sum_own + nn(turned[:, total:], other[:, cols])).astype(BF16)


def up_grad_kernel(normed_own, normed_other, own, other, keep, send, turned):
    total = normed_own.shape[0]
    turned[:, :total] = normed_own[...].T
    turned[:, total:] = normed_other[...].T
    width = keep.shape[1]
    for r, place in enumerate((keep, send)):
        cols = slice(r * width, (r + 1) * width)
        sum_own = nn(turned[:, :total], own[:, cols])
        place[...] = (sum_own + nn(turned[:, total:], other[:, cols])).astype(BF16)


def late_grad_kernel(
    normed_own, normed_other, own, other, o_own, o_other, dattn_own, dattn_other,
    sums_own, sums_other, keep, send, turned,
):
    total, width = normed_own.shape
    base = 3 * width
    last = base + width
    places = (keep, send)
    turned[:, :total] = normed_own[...].T
    turned[:, total:] = normed_other[...].T
    for c in range(3):
        whole = nn(turned[:, :total], own[c]) + nn(turned[:, total:], other[c])
        for r, place in enumerate(places):
            cols = slice(r * LANES, (r + 1) * LANES)
            place[c * width : (c + 1) * width, :] = whole[:, cols].astype(BF16)
    for r, place in enumerate(places):
        here = o_own[:, 2 * r * LANES : (2 * r + 1) * LANES].T
        there = o_other[:, r * LANES : (r + 1) * LANES].T
        whole = (nn(here, dattn_own[...]) + nn(there, dattn_other[...])).astype(BF16)
        for n in range(width // LANES):
            to = base + n * LANES
            place[to : to + LANES, :] = whole[:, n * LANES : (n + 1) * LANES]
    four = sums_own[0:4, :] + sums_other[0:4, :]
    small = jnp.concatenate(
        [four[v : v + 1, n * LANES : (n + 1) * LANES] for v in range(4) for n in range(width // LANES)],
        axis=0,
    ).astype(BF16)
    for place in places:
        place[last : last + small.shape[0], :] = small
        left = place.shape[0] - last - small.shape[0]
        place[last + small.shape[0] :, :] = jnp.zeros((left, LANES), BF16)


def unpack_late(source, qkv, out, gains, biases):
    width = out.shape[1]
    base = 3 * width
    last = base + width
    pairs = width // LANES
    for c in range(3):
        qkv[c] = source[c * width : (c + 1) * width, :].astype(F32)
    for n in range(pairs):
        cols = slice(n * LANES, (n + 1) * LANES)
        out[:, cols] = source[base + n * LANES : base + (n + 1) * LANES, :].astype(F32)
        for v, place in enumerate((gains, gains, biases, biases)):
            row = last + v * pairs + n
            place[v % 2 : v % 2 + 1, cols] = source[row : row + 1, :].astype(F32)


def join_late_kernel(where, own, came, qkv, out, gains, biases, whole):
    whole_kernel(where, own, came, whole)
    unpack_late(whole, qkv, out, gains, biases)


def unpack_late_kernel(source, qkv, out, gains, biases, whole):
    whole[...] = source[...].astype(F32)
    unpack_late(whole, qkv, out, gains, biases)


def my_half(where):
    depth = where[DEPTH]
    return (depth ^ (depth >> 1)) & 1


def rows_at(index, size):
    return pl.ds(pl.multiple_of(index * size, 16), size)


def halve_kernel(where, keep, came, stays, goes):
    mine = my_half(where)
    size = stays.shape[0]
    for index, out in ((mine, stays), (1 - mine, goes)):
        rows = rows_at(index, size)
        out[...] = (keep[rows, :].astype(F32) + came[rows, :].astype(F32)).astype(out.dtype)


def sum_kernel(keep, came, out):
    out[...] = (keep[...].astype(F32) + came[...].astype(F32)).astype(BF16)


def whole_kernel(where, own, came, out):
    mine = my_half(where)
    size = own.shape[0]
    out[rows_at(mine, size), :] = own[...].astype(F32)
    out[rows_at(1 - mine, size), :] = came[...].astype(F32)


def put_rows(place, part, out, rms, row_of):
    total, width = part.shape
    begin = place * (total // LANES)

    @pl.loop(0, total // LANES, unroll=True)
    def _(tile):
        block = part[pl.ds(pl.multiple_of(tile * LANES, LANES), LANES), :].astype(F32)
        out[pl.ds(pl.multiple_of((row_of + tile) * LANES, LANES), LANES), :] = block
        if rms is not None:
            square = block * block
            high = square.astype(BF16)
            low = (square - high.astype(F32)).astype(BF16)
            ones = jnp.ones((width, LANES), BF16)
            mean = (nn(high, ones) + nn(low, ones)) * (1.0 / width)
            row = lax.broadcasted_iota(jnp.int32, (LANES, LANES), 0)
            col = lax.broadcasted_iota(jnp.int32, (LANES, LANES), 1)
            mean = jnp.sum(jnp.where(row == col, mean, 0.0), axis=0, keepdims=True)
            rms[pl.ds(begin + tile, 1), :] = jnp.sqrt(mean + 1e-06)


def finish_kernel(where, p0, p1, p2, p3, out):
    for r, part in enumerate((p0, p1, p2, p3)):
        place = where[PLACE] ^ r
        put_rows(place, part, out, None, place * (part.shape[0] // LANES))


def most_kernel(where, p0, p1, p2, out, rms):
    for r, part in enumerate((p0, p1, p2)):
        place = where[PLACE] ^ r
        put_rows(place, part, out, rms, place * (part.shape[0] // LANES))


def rest_kernel(where, p3, rms_most, most, out, rms, block, sem):
    del most
    rms[...] = rms_most[...]
    total = p3.shape[0]
    place = where[PLACE] ^ 3
    put_rows(place, p3, block, rms, 0)
    to = out.at[pl.ds(pl.multiple_of(place * total, total), total), :]
    copy = pltpu.make_async_copy(block, to, sem)
    copy.start()
    copy.wait()


IN_VMEM = pl.BlockSpec(memory_space=pltpu.VMEM)
IN_SMEM = pl.BlockSpec(memory_space=pltpu.SMEM)
ANYWHERE = pl.BlockSpec(memory_space=pl.ANY)


def call(kernel, operands, outputs, scratch, name, us, far=(), in_place=False):
    near = [jax.ShapeDtypeStruct(shape, dtype) for shape, dtype in outputs]
    return pl.pallas_call(
        kernel,
        out_shape=near,
        in_specs=[IN_SMEM if v.dtype == jnp.int32 else IN_VMEM for v in operands]
        + [ANYWHERE] * len(far),
        out_specs=[ANYWHERE] * in_place + [IN_VMEM] * (len(near) - in_place),
        input_output_aliases={len(operands): 0} if in_place else {},
        scratch_shapes=scratch,
        compiler_params=pltpu.CompilerParams(vmem_limit_bytes=VMEM_LIMIT),
        cost_estimate=pl.CostEstimate(
            flops=int(us * 1.1e9), bytes_accessed=0, transcendentals=0
        ),
        name=name,
    )(*operands, *far)


def across(block, distance, axis="head"):
    size = lax.axis_size(axis)
    return lax.ppermute(block, axis, [(i, i ^ distance) for i in range(size)])


def spread(block, far):
    return (block, across(block, 1), far, across(far, 1))


def after(value, *others):
    return lax.optimization_barrier((value, *others))[0]


def sum_over_dp(keep, came, where, name, join):
    rows, width = keep.shape
    if lax.axis_size("dp") != 4:
        total = (keep.astype(F32) + came.astype(F32)).astype(BF16)
        return join(lax.psum(total, "dp"))
    half = (rows // 2, width)
    stays, goes = call(
        halve_kernel, (where, keep, came), [(half, F32), (half, BF16)], [], "halve_" + name, 0.8
    )
    (own,) = call(
        sum_kernel, (stays, across(goes, 1, "dp")), [(half, BF16)], [], "sum_near_" + name, 0.7
    )
    (own,) = call(
        sum_kernel, (own, across(own, 3, "dp")), [(half, BF16)], [], "sum_far_" + name, 0.7
    )
    return join(where, own, across(own, 1, "dp"))


def finish(where, own, far, name):
    shape = (own.shape[0] * 4, own.shape[1])
    operands = (where, own, across(own, 1), far, across(far, 1))
    return call(finish_kernel, operands, [(shape, F32)], [], name, 3.0)[0]


def token_table(segment_start, pad_mask, place, tokens, parts):
    row_count = segment_start.shape[0] // SEQ
    ids = jnp.cumsum(segment_start.reshape(row_count, SEQ), axis=1).reshape(-1)
    begin = place * tokens
    own = lax.dynamic_slice(ids, (begin,), (tokens,))
    before = lax.dynamic_slice(ids, (jnp.maximum(begin - 1, 0),), (1,))
    before = jnp.where(place % parts == 0, jnp.full_like(before, -1), before)
    last = own.reshape(-1, CHUNK)[:, -1]
    previous = jnp.concatenate([before, last[:-1]])
    pad = lax.dynamic_slice(pad_mask, (begin,), (tokens,))
    columns = [
        pad,
        own,
        own == before,
        own == last[-1:],
        own == jnp.repeat(previous, CHUNK),
        own == jnp.repeat(last, CHUNK),
    ]
    columns = jnp.stack([c.astype(F32) for c in columns], axis=1)
    rows = jnp.broadcast_to(own.astype(F32)[None], (8, tokens))
    return columns, rows


def local(
    block_input, cotangent, segment_start, pad_mask, qkv_weight, out_weight, up_weight,
    down_weight, norm_gain, norm_bias,
):
    heads = lax.axis_size("head")
    row_count = block_input.shape[0] // SEQ
    parts = heads // row_count
    assert heads == 4 and parts == 2
    tokens = block_input.shape[0] // heads
    width = block_input.shape[1]
    units = up_weight.shape[-1] * heads
    pairs = width // LANES
    chunks = tokens // CHUNK
    section = lax.axis_index("section")
    place = lax.axis_index("head")

    gain, bias = norm_gain[0], norm_bias[0]
    far_out = across(out_weight[0], 2)
    far_up = across(up_weight[0], 2)
    far_down = across(down_weight[0], 2)

    cols, seg = token_table(segment_start, pad_mask, place, tokens, parts)
    own_x = lax.dynamic_slice(block_input, (place * tokens, 0), (tokens, width))

    wide = (tokens, width)
    state_shape = (pairs, LANES, PAIR)
    dma = pltpu.SemaphoreType.DMA
    mask_shape = ((chunks, CHUNK, 2 * CHUNK), BF16)
    mask_mem = pltpu.VMEM(*mask_shape)
    row_mem = pltpu.VMEM(wide, BF16)

    own_g = lax.dynamic_slice(cotangent, (place * tokens, 0), (tokens, width))
    other_g = lax.dynamic_slice(cotangent, ((place ^ 1) * tokens, 0), (tokens, width))
    where = jnp.stack([section, place, lax.axis_index("dp")]).astype(jnp.int32)
    turned_mem = pltpu.VMEM((width, 2 * tokens), BF16)
    grad_mem = pltpu.VMEM(wide, F32)
    half = (tokens, units // 2)
    features = [(wide, BF16)] * 3 + [(state_shape, BF16)]

    fq, fk, vv, state, qkv = call(
        functools.partial(qkv_kernel, False),
        (where, after(own_x, own_g, other_g, seg), gain, bias, cols),
        features + [((3, width, width), BF16)],
        [row_mem, dma((4,))], "qkv_first", 4.0, far=spread(qkv_weight[0], across(qkv_weight[0], 2)),
    )
    start = across(state, 1)
    mid, normed_two, out_w = call(
        attention_kernel, (fq, fk, vv, start, cols, seg, own_x, gain, bias),
        [(wide, F32), (wide, BF16), ((width, width), BF16)],
        [mask_mem, row_mem, dma((4,))], "attention_first", 5.5,
        far=spread(out_weight[0], after(far_out, fq)),
    )
    up_w = spread(up_weight[0], after(far_up, fq))
    (active,) = call(
        up_kernel, (normed_two, *up_w), [((tokens, units), BF16)], [], "up_first", 3.2
    )
    down_w = spread(down_weight[0], after(far_down, active))
    (y,) = call(down_kernel, (mid, active, *down_w), [(wide, BF16)], [], "down_first", 2.8)
    came = across(y, 1, "section")

    fq, fk, vv, state, normed, x = call(
        functools.partial(qkv_kernel, True), (where, own_x, came, gain, bias, cols, qkv),
        features + [(wide, BF16)] * 2, [], "qkv_second", 3.5,
    )
    start = across(state, 1)
    y, mid, o, o_send, inv_den, states, active, active_send, slope, normed_two, *masks = call(
        block_kernel, (fq, fk, vv, start, cols, seg, x, gain, bias, out_w, *up_w, *down_w),
        [
            (wide, BF16), (wide, F32), (wide, BF16), ((tokens, width // 2), BF16), (wide, F32),
            ((pairs, chunks, LANES, PAIR), BF16), (half, BF16), (half, BF16),
            ((tokens, units), BF16), (wide, BF16), mask_shape, mask_shape,
        ],
        [], "block_second", 10.0,
    )
    far_y = across(y, 2)
    active_two = across(active_send, 1)
    normed_other = across(normed, 1)
    normed_two_other = across(normed_two, 1)
    o_other = across(o_send, 1)

    def attention_back(sums, grad_mid, dnum, dden, end, name):
        third = ((3, tokens, width // 2), BF16)
        extra = [third, third, ((8, width), F32)] if sums else []
        return call(
            functools.partial(attention_back_kernel, bool(sums)),
            (fq, fk, vv, dnum, dden, states, end, cols, *masks, x, grad_mid, gain, qkv, *sums),
            [(wide, BF16)] + extra,
            [grad_mem, pltpu.VMEM((3, *wide), BF16)], name, (LOW if sums else 1.0) * 7.5,
        )

    back_shapes = [(wide, F32), (wide, BF16), (wide, BF16), (state_shape, BF16)]
    back_operands = (slope, mid, o, inv_den, fq, cols, gain, out_w, *up_w, *down_w)
    grad_mid, dnum, dden, moved = call(
        functools.partial(ffn_back_kernel, False), (where, own_g, *back_operands),
        back_shapes, [row_mem], "ffn_back_first", 4.2,
    )
    (grad_x,) = attention_back((), grad_mid, dnum, dden, across(moved, 1), "attention_back_first")
    came = across(grad_x, 1, "section")
    rows = block_input.shape[0]
    whole_outputs = [((rows, width), F32), ((rows // LANES, LANES), F32)]
    most, rms_most = call(
        most_kernel, (where, after(y, grad_x), across(y, 1), far_y), whole_outputs, [],
        "activations_most", 2.8,
    )
    came = after(came, most)

    share = (width, units // 4)
    grad_mid, dnum, dden, moved, dattn, dup, dup_send, sums_two = call(
        functools.partial(ffn_back_kernel, True),
        (where, own_g, came, *back_operands),
        back_shapes + [(wide, BF16), (half, BF16), (half, BF16), ((2, width), F32)],
        [grad_mem], "ffn_back_second", LOW * 5.0,
    )
    dup_other = across(dup_send, 1)
    came_two = across(came, 1)
    end = across(moved, 1)
    keep, send = call(
        down_grad_kernel, (where, own_g, other_g, came, after(came_two, moved), active, active_two),
        [(share, BF16)] * 2, [turned_mem], "down_grad", LOW * 2.2,
    )
    down_keep, down_far = keep, across(send, 2)
    dattn_other = across(dattn, 1)
    grad_x, dproj, dproj_send, sums = attention_back(
        (sums_two,), grad_mid, dnum, dden, after(end, send), "attention_back_second"
    )
    dproj_other = across(dproj_send, 1)
    keep, send = call(
        up_grad_kernel,
        (normed_two, normed_two_other, dup, after(dup_other, grad_x, down_far)),
        [(share, BF16)] * 2, [turned_mem], "up_grad", 1.3,
    )
    up_keep, up_far = keep, across(send, 2)
    dproj_other = after(dproj_other, send)
    late = (4 * width + 64, LANES)
    keep, send = call(
        late_grad_kernel,
        (
            normed, normed_other, dproj, dproj_other, o, o_other, dattn, dattn_other,
            sums, across(sums, 1),
        ),
        [(late, BF16)] * 2, [turned_mem], "late_grad", 1.3,
    )
    late_far = across(send, 2)
    def join_plain(*parts):
        if len(parts) == 1:
            return parts[0].astype(F32)
        return call(whole_kernel, parts, [(share, F32)], [], "whole", 1.5)[0]

    def join_late(*parts):
        results = [
            ((3, width, LANES), F32), ((LANES, width), F32), ((2, width), F32), ((2, width), F32)
        ]
        kernel = unpack_late_kernel if len(parts) == 1 else join_late_kernel
        return call(kernel, parts, results, [pltpu.VMEM(late, F32)], "join_late", 1.5)

    down_total = sum_over_dp(down_keep, after(down_far, send), where, "down", join_plain)
    up_total = sum_over_dp(up_keep, up_far, where, "up", join_plain)
    qkv_total, out_total, gain_total, bias_total = sum_over_dp(
        keep, late_far, where, "late", join_late
    )
    activations, token_rms = call(
        rest_kernel, (where, after(across(far_y, 1), down_total), rms_most), whole_outputs,
        [grad_mem, dma(())], "activations_rest", 1.0, far=(most,), in_place=True,
    )
    own = after(grad_x, send)
    input_grad = finish(where, own, across(own, 2), "input_grad")
    return (
        activations[None], input_grad[None], token_rms.reshape(1, -1), qkv_total[None],
        out_total[None], up_total[None], down_total[None], gain_total[None], bias_total[None],
    )


def solution(mesh):
    placed = (
        P("dp", None),
        P("dp", None),
        P("dp"),
        P("dp"),
        P("section", None, None, "head"),
        P("section", "head", None),
        P("section", None, "head"),
        P("section", None, "head"),
        P("section", None, None),
        P("section", None, None),
    )
    return jax.shard_map(
        local,
        mesh=mesh,
        in_specs=placed,
        out_specs=(
            P("section", "dp", None),
            P("section", "dp", None),
            P("section", "dp"),
            P("section", None, None, "head"),
            P("section", "head", None),
            P("section", None, "head"),
            P("section", None, "head"),
            P("section", None, None),
            P("section", None, None),
        ),
        check_vma=False,
    )
```

```python
import functools

import jax
import jax.numpy as jnp
from jax import lax
from jax.experimental import pallas as pl
from jax.experimental.pallas import tpu as pltpu
from jax.sharding import PartitionSpec as P

E = 64
SEQ = 1024
LANES = 128
PAIR = 2 * LANES
CHUNK = 256
EPS = 1e-05
F32 = jnp.float32
BF16 = jnp.bfloat16
ROWS = 128
GELU_C = 0.7978845608028654
GELU_A = 0.044715
SPLIT = 1.0 / 32.0
LOW = 0.02
VMEM_LIMIT = 16 * 1024 * 1024

SECTION, PLACE, DEPTH = range(3)

PAD, SEG, CARRY_IN, TAIL_OUT, CARRIED, TAIL = range(6)


def nn(a, b):
    return jnp.dot(a, b, preferred_element_type=F32)


def nt(a, b):
    return lax.dot_general(a, b, (((1,), (1,)), ((), ())), preferred_element_type=F32)


def tn(a, b):
    return lax.dot_general(a, b, (((0,), (0,)), ((), ())), preferred_element_type=F32)


def first_head(shape):
    return lax.broadcasted_iota(jnp.int32, shape, len(shape) - 1) % LANES < E


def diagonal_blocks():
    row = lax.broadcasted_iota(jnp.int32, (LANES, PAIR), 0) < E
    return (row == first_head((LANES, PAIR))).astype(F32)


def split_pair(block):
    in_a = first_head(block.shape)
    zero = jnp.zeros_like(block)
    return jnp.concatenate([jnp.where(in_a, block, zero), jnp.where(in_a, zero, block)], axis=0)


def side(block, fill):
    return jnp.concatenate([block, jnp.full(block.shape, fill, block.dtype)], axis=1)


def normalise(values):
    centre = jnp.mean(values, axis=-1, keepdims=True)
    shifted = values - centre
    scale = lax.rsqrt(jnp.mean(shifted * shifted, axis=-1, keepdims=True) + EPS)
    return shifted * scale, scale


def norm_backward(grad, unit, scale, gain):
    grad_unit = grad * gain
    mean_grad = jnp.mean(grad_unit, axis=-1, keepdims=True)
    mean_dot = jnp.mean(grad_unit * unit, axis=-1, keepdims=True)
    return scale * (grad_unit - mean_grad - unit * mean_dot)


def row_tiles(total, step=ROWS):
    def decorate(body):
        pl.loop(0, total // step, unroll=True)(
            lambda index: body(pl.ds(pl.multiple_of(index * step, step), step))
        )

    return decorate


def start_copies(parts, place, sems, base):
    copies = [
        pltpu.make_async_copy(part, place(r), sems.at[base + r]) for r, part in enumerate(parts)
    ]
    for copy in copies:
        copy.start()
    return copies


def chunk_masks(cols_ref, seg_ref, mask, mask_t):
    row = lax.broadcasted_iota(jnp.int32, (CHUNK, CHUNK), 0)
    col = lax.broadcasted_iota(jnp.int32, (CHUNK, CHUNK), 1)
    for chunk in range(cols_ref.shape[0] // CHUNK):
        span = slice(chunk * CHUNK, (chunk + 1) * CHUNK)
        same = cols_ref[span, SEG : SEG + 1] == seg_ref[0:1, span]
        if mask is not None:
            lower = (same & (col <= row)).astype(F32).astype(BF16)
            mask[chunk] = jnp.concatenate([lower, lower], axis=1)
        if mask_t is not None:
            upper = (same & (row <= col)).astype(F32).astype(BF16)
            mask_t[chunk] = jnp.concatenate([upper, upper], axis=1)


def qkv_kernel(second, where, own, *rest):
    if second:
        came, gain, bias, cols, w, fq, fk, vv, state, normed, x_out = rest
        copies = []
    else:
        gain, bias, cols, w0, w1, w2, w3, fq, fk, vv, state, w, normed, sems = rest
        copies = start_copies(
            (w0, w1, w2, w3), lambda r: w.at[:, :, r * LANES : (r + 1) * LANES], sems, 0
        )
    total = own.shape[0]

    @row_tiles(total)
    def _(rows):
        x = own[rows, :].astype(F32)
        if second:
            x = jnp.where(where[SECTION] == 0, x, came[rows, :].astype(F32))
            x_out[rows, :] = x.astype(BF16)
        unit, _ = normalise(x)
        normed[rows, :] = (unit * gain[0:1, :] + bias[0:1, :]).astype(BF16)

    for copy in copies:
        copy.wait()

    @row_tiles(total, 256)
    def _(rows):
        block = normed[rows, :]
        query = nn(block, w[0])
        fq[rows, :] = jnp.where(query > 0, query + 1.0, jnp.exp(jnp.minimum(query, 0.0))).astype(BF16)
        key = nn(block, w[1])
        key = jnp.where(key > 0, key + 1.0, jnp.exp(jnp.minimum(key, 0.0)))
        fk[rows, :] = (key * cols[rows, PAD : PAD + 1]).astype(BF16)
        vv[rows, :] = nn(block, w[2]).astype(BF16)

    diag = diagonal_blocks()
    for pair in range(state.shape[0]):
        lanes = slice(pair * LANES, (pair + 1) * LANES)
        tail = (fk[:, lanes] * cols[:, TAIL_OUT : TAIL_OUT + 1].astype(BF16)).astype(BF16)
        state[pair] = (diag * tn(tail, side(vv[:, lanes], 1.0))).astype(BF16)


def attention_forward(fq, fk, vv, start, cols, o, inv_den, states, mask):
    diag = diagonal_blocks()

    for pair in range(start.shape[0]):
        lanes = slice(pair * LANES, (pair + 1) * LANES)
        state = start[pair ^ 1].astype(F32)
        for chunk in range(fq.shape[0] // CHUNK):
            span = slice(chunk * CHUNK, (chunk + 1) * CHUNK)
            query, key, value = fq[span, lanes], fk[span, lanes], vv[span, lanes]
            carried = cols[span, CARRIED : CARRIED + 1]
            tail = cols[span, TAIL : TAIL + 1].astype(BF16)
            state_low = state.astype(BF16)
            if states is not None:
                states[pair, chunk] = state_low
            scores = nt(query, split_pair(key)).astype(BF16) * mask[chunk]
            ones = split_pair(jnp.ones_like(value))
            values = jnp.concatenate([split_pair(value), ones], axis=1)
            both = nn(scores, values) + carried * nn(query, state_low)
            inverse = 1.0 / (both[:, LANES:] + 1.0)
            o[span, lanes] = (both[:, :LANES] * inverse).astype(BF16)
            if inv_den is not None:
                inv_den[span, lanes] = inverse
            keep = carried[CHUNK - 1 : CHUNK, :]
            state = keep * state + diag * tn(key * tail, side(value, 1.0))


def out_and_norm(o, x, out_w, gain, bias, mid, normed_two):
    @row_tiles(o.shape[0], 256)
    def _(rows):
        mid[rows, :] = x[rows, :].astype(F32) + nn(o[rows, :], out_w[...])

    @row_tiles(o.shape[0])
    def _(rows):
        unit, _ = normalise(mid[rows, :])
        normed_two[rows, :] = (unit * gain[1:2, :] + bias[1:2, :]).astype(BF16)


def gelu_parts(up, with_slope):
    half = 0.5 + 0.5 * jnp.tanh(up * (GELU_C + GELU_C * GELU_A * (up * up)))
    half, up = half.astype(BF16), up.astype(BF16)
    value = up * half
    if not with_slope:
        return value, None
    slope = 2 * GELU_C + 6 * GELU_C * GELU_A * (up * up)
    return value, half + value * (1.0 - half) * slope


def attention_kernel(
    fq, fk, vv, start, cols, seg, x, gain, bias, w0, w1, w2, w3, mid, normed_two, w, mask, o, sems
):
    copies = start_copies(
        (w0, w1, w2, w3), lambda r: w.at[r * LANES : (r + 1) * LANES, :], sems, 0
    )
    chunk_masks(cols, seg, mask, None)
    attention_forward(fq, fk, vv, start, cols, o, None, None, mask)
    for copy in copies:
        copy.wait()
    out_and_norm(o, x, w, gain, bias, mid, normed_two)


def up_kernel(normed_two, w0, w1, w2, w3, active):
    width = w0.shape[1]
    for r, w in enumerate((w0, w1, w2, w3)):

        @row_tiles(normed_two.shape[0], 256)
        def _(rows, r=r, w=w):
            up = nn(normed_two[rows, :], w[...])
            active[rows, r * width : (r + 1) * width] = gelu_parts(up, False)[0]


def down_kernel(mid, active, w0, w1, w2, w3, y):
    width = w0.shape[1]

    @row_tiles(mid.shape[0], 256)
    def _(rows):
        total = mid[rows, :]
        for r, w in enumerate((w0, w1, w2, w3)):
            total = total + nt(active[rows, r * width : (r + 1) * width], w[...])
        y[rows, :] = total.astype(BF16)


def block_kernel(
    fq, fk, vv, start, cols, seg, x, gain, bias, out_w, u0, u1, u2, u3, d0, d1, d2, d3,
    y, mid, o, o_send, inv_den, states, keep, send, slope, normed_two, mask, mask_t,
):
    chunk_masks(cols, seg, mask, mask_t)
    attention_forward(fq, fk, vv, start, cols, o, inv_den, states, mask)
    for slot, r in enumerate((1, 3)):
        o_send[:, slot * LANES : (slot + 1) * LANES] = o[:, r * LANES : (r + 1) * LANES]
    out_and_norm(o, x, out_w, gain, bias, mid, normed_two)
    up_w, down_w = (u0, u1, u2, u3), (d0, d1, d2, d3)
    width = u0.shape[1]

    @row_tiles(x.shape[0], 512)
    def _(rows):
        total = mid[rows, :]
        for r in range(4):
            units = slice(r * width, (r + 1) * width)
            value, steep = gelu_parts(nn(normed_two[rows, :], up_w[r][...]), True)
            half = slice(r // 2 * width, (r // 2 + 1) * width)
            (send if r % 2 else keep)[rows, half] = value
            slope[rows, units] = steep
            total = total + nt(value, down_w[r][...])
        y[rows, :] = total.astype(BF16)


def ffn_rows(rows, gy, slope, up_w, down_w, save):
    width = up_w[0].shape[1]
    dffn = gy[rows, :].astype(BF16)
    grad = jnp.zeros(dffn.shape, F32)
    for r in range(4):
        units = slice(r * width, (r + 1) * width)
        dup = slope[rows, units] * nn(dffn, down_w[r][...]).astype(BF16)
        if save is not None:
            half = slice(r // 2 * width, (r // 2 + 1) * width)
            save[r % 2][rows, half] = dup
        grad = grad + nt(dup, up_w[r][...])
    return grad


def ffn_back_kernel(second, where, own_g, *rest):
    if second:
        came, rest = rest[0], rest[1:]
    slope, mid, o, inv_den, fq, cols, gain, out_w, *rest = rest
    up_w, down_w = rest[0:4], rest[4:8]
    grad_mid, dnum, dden, grad_state, dattn, *rest = rest[8:]
    gy, save, sums = own_g, None, None
    if second:
        *save, sums, gy = rest

        @row_tiles(gy.shape[0])
        def _(rows):
            gy[rows, :] = jnp.where(
                where[SECTION] == 1, own_g[rows, :], came[rows, :].astype(F32)
            )

    @row_tiles(gy.shape[0], 512)
    def _(rows):
        grad_mid[rows, :] = ffn_rows(rows, gy, slope, up_w, down_w, save)

    mid_back(
        gy, mid, o, inv_den, fq, cols, gain, out_w, grad_mid, dnum, dden, grad_state, dattn, sums
    )


def mid_back(
    gy, mid, o, inv_den, fq, cols, gain, out_w, grad_mid, dnum, dden, grad_state, dattn, sums
):
    total = gy.shape[0]
    if sums is not None:
        sums[...] = jnp.zeros_like(sums)

    @row_tiles(total)
    def _(rows):
        unit, scale = normalise(mid[rows, :])
        grad = grad_mid[rows, :]
        if sums is not None:
            sums[0:1, :] += jnp.sum(grad * unit, axis=0, keepdims=True)
            sums[1:2, :] += jnp.sum(grad, axis=0, keepdims=True)
        grad = gy[rows, :] + norm_backward(grad, unit, scale, gain[1:2, :])
        grad_mid[rows, :] = grad
        dattn[rows, :] = grad.astype(BF16)

    row_a = lax.broadcasted_iota(jnp.int32, (LANES, LANES), 0) < E
    spread = (row_a == first_head((LANES, LANES))).astype(BF16)
    use_low = lax.broadcasted_iota(jnp.int32, (512, LANES), 1) % E >= E // 2

    @row_tiles(total, 512)
    def _(rows):
        grad_heads = nt(dattn[rows, :], out_w[...])
        scaled = grad_heads * inv_den[rows, :]
        dnum[rows, :] = scaled.astype(BF16)
        product = -scaled * o[rows, :].astype(F32)
        for pair in range(grad_state.shape[0]):
            lanes = slice(pair * LANES, (pair + 1) * LANES)
            part = product[:, lanes]
            high = part.astype(BF16)
            low = (part - high.astype(F32)).astype(BF16)
            whole = nn(high, spread) + nn(low, spread)
            high = whole.astype(BF16)
            low = (whole - high.astype(F32)).astype(BF16)
            dden[rows, lanes] = jnp.where(use_low, low, high)

    diag = diagonal_blocks()
    carry_in = cols[:, CARRY_IN : CARRY_IN + 1].astype(BF16)
    for pair in range(grad_state.shape[0]):
        lanes = slice(pair * LANES, (pair + 1) * LANES)
        both = jnp.concatenate([dnum[:, lanes], dden[:, lanes]], axis=1)
        grad_state[pair] = (diag * tn(fq[:, lanes] * carry_in, both)).astype(BF16)


def attention_back_kernel(
    with_weights, fq, fk, vv, dnum, dden, states, end, cols, mask, mask_t, x, grad_mid, gain, w, *rest
):
    if with_weights:
        sums_two, grad_x, keep, send, sums, *rest = rest
    else:
        grad_x, *rest = rest
    acc, dproj = rest
    diag = diagonal_blocks()
    lane = lax.broadcasted_iota(jnp.int32, (1, PAIR), 1)
    share = jnp.where(lane < LANES, 1.0, SPLIT)

    for pair in range(end.shape[0]):
        lanes = slice(pair * LANES, (pair + 1) * LANES)
        grad_state = end[pair ^ 1].astype(F32)
        for chunk in reversed(range(fq.shape[0] // CHUNK)):
            span = slice(chunk * CHUNK, (chunk + 1) * CHUNK)
            query, key, value = fq[span, lanes], fk[span, lanes], vv[span, lanes]
            grad_n, grad_d = dnum[span, lanes], dden[span, lanes]
            carried = cols[span, CARRIED : CARRIED + 1]
            tail = cols[span, TAIL : TAIL + 1]
            stays = carried[CHUNK - 1 : CHUNK, :]
            query_two = split_pair(query)
            grad_n_two = split_pair(grad_n)
            both = jnp.concatenate([grad_n, grad_d], axis=1)
            both_two = jnp.concatenate([grad_n_two, split_pair(grad_d)], axis=1)
            share_two = split_pair(jnp.full(value.shape, SPLIT, BF16))
            values_two = jnp.concatenate([split_pair(value), share_two], axis=1)
            values = side(value, SPLIT)
            scores_t = nt(key, query_two).astype(BF16) * mask_t[chunk]
            dscores = nt(both, values_two).astype(BF16) * mask[chunk]
            dscores_t = nt(values, both_two).astype(BF16) * mask_t[chunk]
            state = (states[pair, chunk].astype(F32) * share).astype(BF16)
            grad_low = grad_state.astype(BF16)
            dfq = nn(dscores, split_pair(key)) + carried * nt(both, state)
            dfk = nn(dscores_t, query_two) + tail * nt(values, grad_low)
            dvv = nn(scores_t, grad_n_two) + tail * nn(key, grad_low[:, :LANES])
            dproj[0, span, lanes] = (jnp.minimum(query.astype(F32), 1.0) * dfq).astype(BF16)
            dproj[1, span, lanes] = (jnp.minimum(key.astype(F32), 1.0) * dfk).astype(BF16)
            dproj[2, span, lanes] = dvv.astype(BF16)
            moved = diag * tn(query * carried.astype(BF16), both)
            grad_state = stays * grad_state + moved

    @row_tiles(x.shape[0], 256)
    def _(rows):
        acc[rows, :] = (
            nt(dproj[0, rows, :], w[0]) + nt(dproj[1, rows, :], w[1]) + nt(dproj[2, rows, :], w[2])
        )

    if with_weights:
        for r in range(4):
            half = slice(r // 2 * LANES, (r // 2 + 1) * LANES)
            (send if r % 2 else keep)[:, :, half] = dproj[:, :, r * LANES : (r + 1) * LANES]
        sums[...] = jnp.zeros_like(sums)
        sums[1:2, :] = sums_two[0:1, :]
        sums[3:4, :] = sums_two[1:2, :]

    @row_tiles(x.shape[0])
    def _(rows):
        unit, scale = normalise(x[rows, :].astype(F32))
        grad = acc[rows, :]
        if with_weights:
            sums[0:1, :] += jnp.sum(grad * unit, axis=0, keepdims=True)
            sums[2:3, :] += jnp.sum(grad, axis=0, keepdims=True)
        grad = grad_mid[rows, :] + norm_backward(grad, unit, scale, gain[0:1, :])
        grad_x[rows, :] = grad.astype(BF16)


def down_grad_kernel(where, own_g, other_g, came, came_two, own, other, keep, send, turned):
    total = own_g.shape[0]
    for n, (mine, arrived) in enumerate(((own_g, came), (other_g, came_two))):
        whole = jnp.where(where[SECTION] == 1, mine[...], arrived[...].astype(F32))
        turned[:, n * total : (n + 1) * total] = whole.astype(BF16).T
    width = keep.shape[1]
    for r, place in enumerate((keep, send)):
        cols = slice(r * width, (r + 1) * width)
        sum_own = nn(turned[:, :total], own[:, cols])
        place[...] = (sum_own + nn(turned[:, total:], other[:, cols])).astype(BF16)


def up_grad_kernel(normed_own, normed_other, own, other, keep, send, turned):
    total = normed_own.shape[0]
    turned[:, :total] = normed_own[...].T
    turned[:, total:] = normed_other[...].T
    width = keep.shape[1]
    for r, place in enumerate((keep, send)):
        cols = slice(r * width, (r + 1) * width)
        sum_own = nn(turned[:, :total], own[:, cols])
        place[...] = (sum_own + nn(turned[:, total:], other[:, cols])).astype(BF16)


def late_grad_kernel(
    normed_own, normed_other, own, other, o_own, o_other, dattn_own, dattn_other,
    sums_own, sums_other, keep, send, turned,
):
    total, width = normed_own.shape
    base = 3 * width
    last = base + width
    places = (keep, send)
    turned[:, :total] = normed_own[...].T
    turned[:, total:] = normed_other[...].T
    for c in range(3):
        whole = nn(turned[:, :total], own[c]) + nn(turned[:, total:], other[c])
        for r, place in enumerate(places):
            cols = slice(r * LANES, (r + 1) * LANES)
            place[c * width : (c + 1) * width, :] = whole[:, cols].astype(BF16)
    for r, place in enumerate(places):
        here = o_own[:, 2 * r * LANES : (2 * r + 1) * LANES].T
        there = o_other[:, r * LANES : (r + 1) * LANES].T
        whole = (nn(here, dattn_own[...]) + nn(there, dattn_other[...])).astype(BF16)
        for n in range(width // LANES):
            to = base + n * LANES
            place[to : to + LANES, :] = whole[:, n * LANES : (n + 1) * LANES]
    four = sums_own[0:4, :] + sums_other[0:4, :]
    small = jnp.concatenate(
        [four[v : v + 1, n * LANES : (n + 1) * LANES] for v in range(4) for n in range(width // LANES)],
        axis=0,
    ).astype(BF16)
    for place in places:
        place[last : last + small.shape[0], :] = small
        left = place.shape[0] - last - small.shape[0]
        place[last + small.shape[0] :, :] = jnp.zeros((left, LANES), BF16)


def unpack_late(source, qkv, out, gains, biases):
    width = out.shape[1]
    base = 3 * width
    last = base + width
    pairs = width // LANES
    for c in range(3):
        qkv[c] = source[c * width : (c + 1) * width, :].astype(F32)
    for n in range(pairs):
        cols = slice(n * LANES, (n + 1) * LANES)
        out[:, cols] = source[base + n * LANES : base + (n + 1) * LANES, :].astype(F32)
        for v, place in enumerate((gains, gains, biases, biases)):
            row = last + v * pairs + n
            place[v % 2 : v % 2 + 1, cols] = source[row : row + 1, :].astype(F32)


def join_late_kernel(where, own, came, qkv, out, gains, biases, whole):
    whole_kernel(where, own, came, whole)
    unpack_late(whole, qkv, out, gains, biases)


def unpack_late_kernel(source, qkv, out, gains, biases, whole):
    whole[...] = source[...].astype(F32)
    unpack_late(whole, qkv, out, gains, biases)


def my_half(where):
    depth = where[DEPTH]
    return (depth ^ (depth >> 1)) & 1


def rows_at(index, size):
    return pl.ds(pl.multiple_of(index * size, 16), size)


def halve_kernel(where, keep, came, stays, goes):
    mine = my_half(where)
    size = stays.shape[0]
    for index, out in ((mine, stays), (1 - mine, goes)):
        rows = rows_at(index, size)
        out[...] = (keep[rows, :].astype(F32) + came[rows, :].astype(F32)).astype(out.dtype)


def sum_kernel(keep, came, out):
    out[...] = (keep[...].astype(F32) + came[...].astype(F32)).astype(BF16)


def whole_kernel(where, own, came, out):
    mine = my_half(where)
    size = own.shape[0]
    out[rows_at(mine, size), :] = own[...].astype(F32)
    out[rows_at(1 - mine, size), :] = came[...].astype(F32)


def put_rows(place, part, out, rms, row_of):
    total, width = part.shape
    begin = place * (total // LANES)

    @pl.loop(0, total // LANES, unroll=True)
    def _(tile):
        block = part[pl.ds(pl.multiple_of(tile * LANES, LANES), LANES), :].astype(F32)
        out[pl.ds(pl.multiple_of((row_of + tile) * LANES, LANES), LANES), :] = block
        if rms is not None:
            square = block * block
            high = square.astype(BF16)
            low = (square - high.astype(F32)).astype(BF16)
            ones = jnp.ones((width, LANES), BF16)
            mean = (nn(high, ones) + nn(low, ones)) * (1.0 / width)
            row = lax.broadcasted_iota(jnp.int32, (LANES, LANES), 0)
            col = lax.broadcasted_iota(jnp.int32, (LANES, LANES), 1)
            mean = jnp.sum(jnp.where(row == col, mean, 0.0), axis=0, keepdims=True)
            rms[pl.ds(begin + tile, 1), :] = jnp.sqrt(mean + 1e-06)


def finish_kernel(where, p0, p1, p2, p3, out):
    for r, part in enumerate((p0, p1, p2, p3)):
        place = where[PLACE] ^ r
        put_rows(place, part, out, None, place * (part.shape[0] // LANES))


def most_kernel(where, p0, p1, p2, out, rms):
    for r, part in enumerate((p0, p1, p2)):
        place = where[PLACE] ^ r
        put_rows(place, part, out, rms, place * (part.shape[0] // LANES))


def rest_kernel(where, p3, rms_most, most, out, rms, block, sem):
    del most
    rms[...] = rms_most[...]
    total = p3.shape[0]
    place = where[PLACE] ^ 3
    put_rows(place, p3, block, rms, 0)
    to = out.at[pl.ds(pl.multiple_of(place * total, total), total), :]
    copy = pltpu.make_async_copy(block, to, sem)
    copy.start()
    copy.wait()


IN_VMEM = pl.BlockSpec(memory_space=pltpu.VMEM)
IN_SMEM = pl.BlockSpec(memory_space=pltpu.SMEM)
ANYWHERE = pl.BlockSpec(memory_space=pl.ANY)


def call(kernel, operands, outputs, scratch, name, us, far=(), in_place=False):
    near = [jax.ShapeDtypeStruct(shape, dtype) for shape, dtype in outputs]
    return pl.pallas_call(
        kernel,
        out_shape=near,
        in_specs=[IN_SMEM if v.dtype == jnp.int32 else IN_VMEM for v in operands]
        + [ANYWHERE] * len(far),
        out_specs=[ANYWHERE] * in_place + [IN_VMEM] * (len(near) - in_place),
        input_output_aliases={len(operands): 0} if in_place else {},
        scratch_shapes=scratch,
        compiler_params=pltpu.CompilerParams(vmem_limit_bytes=VMEM_LIMIT),
        cost_estimate=pl.CostEstimate(
            flops=int(us * 1.1e9), bytes_accessed=0, transcendentals=0
        ),
        name=name,
    )(*operands, *far)


def across(block, distance, axis="head"):
    size = lax.axis_size(axis)
    return lax.ppermute(block, axis, [(i, i ^ distance) for i in range(size)])


def spread(block, far):
    return (block, across(block, 1), far, across(far, 1))


def after(value, *others):
    return lax.optimization_barrier((value, *others))[0]


def sum_over_dp(keep, came, where, name, join):
    rows, width = keep.shape
    if lax.axis_size("dp") != 4:
        total = (keep.astype(F32) + came.astype(F32)).astype(BF16)
        return join(lax.psum(total, "dp"))
    half = (rows // 2, width)
    stays, goes = call(
        halve_kernel, (where, keep, came), [(half, F32), (half, BF16)], [], "halve_" + name, 0.8
    )
    (own,) = call(
        sum_kernel, (stays, across(goes, 1, "dp")), [(half, BF16)], [], "sum_near_" + name, 0.7
    )
    (own,) = call(
        sum_kernel, (own, across(own, 3, "dp")), [(half, BF16)], [], "sum_far_" + name, 0.7
    )
    return join(where, own, across(own, 1, "dp"))


def finish(where, own, far, name):
    shape = (own.shape[0] * 4, own.shape[1])
    operands = (where, own, across(own, 1), far, across(far, 1))
    return call(finish_kernel, operands, [(shape, F32)], [], name, 3.0)[0]


def token_table(segment_start, pad_mask, place, tokens, parts):
    row_count = segment_start.shape[0] // SEQ
    ids = jnp.cumsum(segment_start.reshape(row_count, SEQ), axis=1).reshape(-1)
    begin = place * tokens
    own = lax.dynamic_slice(ids, (begin,), (tokens,))
    before = lax.dynamic_slice(ids, (jnp.maximum(begin - 1, 0),), (1,))
    before = jnp.where(place % parts == 0, jnp.full_like(before, -1), before)
    last = own.reshape(-1, CHUNK)[:, -1]
    previous = jnp.concatenate([before, last[:-1]])
    pad = lax.dynamic_slice(pad_mask, (begin,), (tokens,))
    columns = [
        pad,
        own,
        own == before,
        own == last[-1:],
        own == jnp.repeat(previous, CHUNK),
        own == jnp.repeat(last, CHUNK),
    ]
    columns = jnp.stack([c.astype(F32) for c in columns], axis=1)
    rows = jnp.broadcast_to(own.astype(F32)[None], (8, tokens))
    return columns, rows


def local(
    block_input, cotangent, segment_start, pad_mask, qkv_weight, out_weight, up_weight,
    down_weight, norm_gain, norm_bias,
):
    heads = lax.axis_size("head")
    row_count = block_input.shape[0] // SEQ
    parts = heads // row_count
    assert heads == 4 and parts == 2
    tokens = block_input.shape[0] // heads
    width = block_input.shape[1]
    units = up_weight.shape[-1] * heads
    pairs = width // LANES
    chunks = tokens // CHUNK
    section = lax.axis_index("section")
    place = lax.axis_index("head")

    gain, bias = norm_gain[0], norm_bias[0]
    far_out = across(out_weight[0], 2)
    far_up = across(up_weight[0], 2)
    far_down = across(down_weight[0], 2)

    cols, seg = token_table(segment_start, pad_mask, place, tokens, parts)
    own_x = lax.dynamic_slice(block_input, (place * tokens, 0), (tokens, width))

    wide = (tokens, width)
    state_shape = (pairs, LANES, PAIR)
    dma = pltpu.SemaphoreType.DMA
    mask_shape = ((chunks, CHUNK, 2 * CHUNK), BF16)
    mask_mem = pltpu.VMEM(*mask_shape)
    row_mem = pltpu.VMEM(wide, BF16)

    own_g = lax.dynamic_slice(cotangent, (place * tokens, 0), (tokens, width))
    other_g = lax.dynamic_slice(cotangent, ((place ^ 1) * tokens, 0), (tokens, width))
    where = jnp.stack([section, place, lax.axis_index("dp")]).astype(jnp.int32)
    turned_mem = pltpu.VMEM((width, 2 * tokens), BF16)
    grad_mem = pltpu.VMEM(wide, F32)
    half = (tokens, units // 2)
    features = [(wide, BF16)] * 3 + [(state_shape, BF16)]

    fq, fk, vv, state, qkv = call(
        functools.partial(qkv_kernel, False),
        (where, after(own_x, own_g, other_g, seg), gain, bias, cols),
        features + [((3, width, width), BF16)],
        [row_mem, dma((4,))], "qkv_first", 4.0, far=spread(qkv_weight[0], across(qkv_weight[0], 2)),
    )
    start = across(state, 1)
    mid, normed_two, out_w = call(
        attention_kernel, (fq, fk, vv, start, cols, seg, own_x, gain, bias),
        [(wide, F32), (wide, BF16), ((width, width), BF16)],
        [mask_mem, row_mem, dma((4,))], "attention_first", 5.5,
        far=spread(out_weight[0], after(far_out, fq)),
    )
    up_w = spread(up_weight[0], after(far_up, fq))
    (active,) = call(
        up_kernel, (normed_two, *up_w), [((tokens, units), BF16)], [], "up_first", 3.2
    )
    down_w = spread(down_weight[0], after(far_down, active))
    (y,) = call(down_kernel, (mid, active, *down_w), [(wide, BF16)], [], "down_first", 2.8)
    came = across(y, 1, "section")

    fq, fk, vv, state, normed, x = call(
        functools.partial(qkv_kernel, True), (where, own_x, came, gain, bias, cols, qkv),
        features + [(wide, BF16)] * 2, [], "qkv_second", 3.5,
    )
    start = across(state, 1)
    y, mid, o, o_send, inv_den, states, active, active_send, slope, normed_two, *masks = call(
        block_kernel, (fq, fk, vv, start, cols, seg, x, gain, bias, out_w, *up_w, *down_w),
        [
            (wide, BF16), (wide, F32), (wide, BF16), ((tokens, width // 2), BF16), (wide, F32),
            ((pairs, chunks, LANES, PAIR), BF16), (half, BF16), (half, BF16),
            ((tokens, units), BF16), (wide, BF16), mask_shape, mask_shape,
        ],
        [], "block_second", 10.0,
    )
    far_y = across(y, 2)
    active_two = across(active_send, 1)
    normed_other = across(normed, 1)
    normed_two_other = across(normed_two, 1)
    o_other = across(o_send, 1)

    def attention_back(sums, grad_mid, dnum, dden, end, name):
        third = ((3, tokens, width // 2), BF16)
        extra = [third, third, ((8, width), F32)] if sums else []
        return call(
            functools.partial(attention_back_kernel, bool(sums)),
            (fq, fk, vv, dnum, dden, states, end, cols, *masks, x, grad_mid, gain, qkv, *sums),
            [(wide, BF16)] + extra,
            [grad_mem, pltpu.VMEM((3, *wide), BF16)], name, (LOW if sums else 1.0) * 7.5,
        )

    back_shapes = [(wide, F32), (wide, BF16), (wide, BF16), (state_shape, BF16)]
    back_operands = (slope, mid, o, inv_den, fq, cols, gain, out_w, *up_w, *down_w)
    grad_mid, dnum, dden, moved = call(
        functools.partial(ffn_back_kernel, False), (where, own_g, *back_operands),
        back_shapes, [row_mem], "ffn_back_first", 4.2,
    )
    (grad_x,) = attention_back((), grad_mid, dnum, dden, across(moved, 1), "attention_back_first")
    came = across(grad_x, 1, "section")
    rows = block_input.shape[0]
    whole_outputs = [((rows, width), F32), ((rows // LANES, LANES), F32)]
    most, rms_most = call(
        most_kernel, (where, after(y, grad_x), across(y, 1), far_y), whole_outputs, [],
        "activations_most", 2.8,
    )
    came = after(came, most)

    share = (width, units // 4)
    grad_mid, dnum, dden, moved, dattn, dup, dup_send, sums_two = call(
        functools.partial(ffn_back_kernel, True),
        (where, own_g, came, *back_operands),
        back_shapes + [(wide, BF16), (half, BF16), (half, BF16), ((2, width), F32)],
        [grad_mem], "ffn_back_second", LOW * 5.0,
    )
    dup_other = across(dup_send, 1)
    came_two = across(came, 1)
    end = across(moved, 1)
    keep, send = call(
        down_grad_kernel, (where, own_g, other_g, came, after(came_two, moved), active, active_two),
        [(share, BF16)] * 2, [turned_mem], "down_grad", LOW * 2.2,
    )
    down_keep, down_far = keep, across(send, 2)
    dattn_other = across(dattn, 1)
    grad_x, dproj, dproj_send, sums = attention_back(
        (sums_two,), grad_mid, dnum, dden, after(end, send), "attention_back_second"
    )
    dproj_other = across(dproj_send, 1)
    keep, send = call(
        up_grad_kernel,
        (normed_two, normed_two_other, dup, after(dup_other, grad_x, down_far)),
        [(share, BF16)] * 2, [turned_mem], "up_grad", 1.3,
    )
    up_keep, up_far = keep, across(send, 2)
    dproj_other = after(dproj_other, send)
    late = (4 * width + 64, LANES)
    keep, send = call(
        late_grad_kernel,
        (
            normed, normed_other, dproj, dproj_other, o, o_other, dattn, dattn_other,
            sums, across(sums, 1),
        ),
        [(late, BF16)] * 2, [turned_mem], "late_grad", 1.3,
    )
    late_far = across(send, 2)
    def join_plain(*parts):
        if len(parts) == 1:
            return parts[0].astype(F32)
        return call(whole_kernel, parts, [(share, F32)], [], "whole", 1.5)[0]

    def join_late(*parts):
        results = [
            ((3, width, LANES), F32), ((LANES, width), F32), ((2, width), F32), ((2, width), F32)
        ]
        kernel = unpack_late_kernel if len(parts) == 1 else join_late_kernel
        return call(kernel, parts, results, [pltpu.VMEM(late, F32)], "join_late", 1.5)

    down_total = sum_over_dp(down_keep, after(down_far, send), where, "down", join_plain)
    up_total = sum_over_dp(up_keep, up_far, where, "up", join_plain)
    qkv_total, out_total, gain_total, bias_total = sum_over_dp(
        keep, late_far, where, "late", join_late
    )
    activations, token_rms = call(
        rest_kernel, (where, after(across(far_y, 1), down_total), rms_most), whole_outputs,
        [grad_mem, dma(())], "activations_rest", 1.0, far=(most,), in_place=True,
    )
    own = after(grad_x, send)
    input_grad = finish(where, own, across(own, 2), "input_grad")
    return (
        activations[None], input_grad[None], token_rms.reshape(1, -1), qkv_total[None],
        out_total[None], up_total[None], down_total[None], gain_total[None], bias_total[None],
    )


def solution(mesh):
    placed = (
        P("dp", None),
        P("dp", None),
        P("dp"),
        P("dp"),
        P("section", None, None, "head"),
        P("section", "head", None),
        P("section", None, "head"),
        P("section", None, "head"),
        P("section", None, None),
        P("section", None, None),
    )
    return jax.shard_map(
        local,
        mesh=mesh,
        in_specs=placed,
        out_specs=(
            P("section", "dp", None),
            P("section", "dp", None),
            P("section", "dp"),
            P("section", None, None, "head"),
            P("section", "head", None),
            P("section", None, "head"),
            P("section", None, "head"),
            P("section", None, None),
            P("section", None, None),
        ),
        check_vma=False,
    )
```
